512 devices in a mesh: dp: 8 (over z_lo), seq: 8 (over z_hi, y), head: 8 (over x, core).
Axes of the slice: x: 4, y: 4, z: 16 (z_hi: 2, z_lo: 8; z = z_hi * 8 + z_lo), core: 2. Of those that a mesh axis runs over, the one named last changes fastest.
Arguments:
- queries: bfloat16 [65536, 4096], P(('dp', 'seq', 'head')), parts along dimension 0, may hold values from -5 to 5
- stored_key_rows: bfloat16 [65536, 512], P(('dp', 'seq', 'head')), parts along dimension 0, may hold values from -5 to 5
- stored_value_rows: bfloat16 [65536, 512], P(('dp', 'seq', 'head')), parts along dimension 0, may hold values from -6 to 6
- grad_out: bfloat16 [65536, 4096], P(('dp', 'seq', 'head')), parts along dimension 0, may hold values from -6 to 6
- segment_ids: int32 [65536], P('dp'), parts along dimension 0, may hold values from 0 to 47, never falling along the last dimension, each value on 1 to 256 neighbouring positions
- stored_block_order: int32 [128], P('dp'), parts along dimension 0, may hold values from 0 to 15, each once
Outputs:
- attended: bfloat16 [65536, 4096], P(('dp', 'seq', 'head')), parts along dimension 0
- grad_query: bfloat16 [65536, 4096], P(('dp', 'seq', 'head')), parts along dimension 0
- key_gradient: bfloat16 [65536, 512], P(('dp', 'seq', 'head')), parts along dimension 0
- value_gradient: bfloat16 [65536, 512], P(('dp', 'seq', 'head')), parts along dimension 0
The draws below stay inside these ranges and needn't reach their ends.
There are 8 independent parts, one for each index of `dp`. The reference program is written for one: setup_inputs(seed, part) draws one part's arguments, and reference() takes and returns one part's arrays. A program takes and returns all parts, laid end to end along the dimension named above; each array names one. Nothing has to cross between parts.
Inputs may be any that keep to these rules, and one draw needn't show every extreme that they name: `segment_ids`: indexed by sequence position, not by stored row; never falls; each document holds at most 256 positions, one exactly 256. Stored block j, rows j * 512 to j * 512 + 511, holds sequence block stored_block_order[j]; each block once.
All inputs are finite; a program needn't handle non-finite values.
Results may differ from the reference program's by a relative error of at most 0.019.
Values may be sent and summed in bfloat16 or wider, within the bound.
No kernel may reach another device: no remote copies, remote signals or barrier semaphores. Data moves between devices by JAX's collectives and lax.ppermute only.
A program may use at most 64 MiB of HBM per device.

```python
import math
import jax
import jax.numpy as jnp
import numpy as np
from jax import lax

HEAD_SIZE = 128
QUERY_HEADS = 32
KEY_VALUE_HEADS = 4
BLOCK = 512
TOKEN_LENGTH = 8192
DOCS = 48
N_SEQ = 8
N_HEAD = 8


def draw_queries(key, part):
    key = jax.random.fold_in(key, 11)
    value_entries = jax.random.truncated_normal(key, -4.0, 4.0, (TOKEN_LENGTH, QUERY_HEADS * HEAD_SIZE), jnp.float32)
    return value_entries.astype(jnp.bfloat16)


def draw_stored_key_rows(key, part):
    key = jax.random.fold_in(key, 23)
    value_entries = jax.random.truncated_normal(key, -4.0, 4.0, (TOKEN_LENGTH, KEY_VALUE_HEADS * HEAD_SIZE), jnp.float32)
    return value_entries.astype(jnp.bfloat16)


def block_levels(key, shape, pieces, low, high):
    def one(axis_at, parts):
        heights = jax.random.uniform(jax.random.fold_in(jax.random.fold_in(key, 6), axis_at), (parts,), jnp.float32, low / len(pieces), high / len(pieces))
        return jnp.repeat(jnp.exp(heights), shape[axis_at] // parts).reshape((-1,) + (1,) * (len(shape) - axis_at - 1))

    factor_of = one(*pieces[0])
    for cut in pieces[1:]:
        factor_of = factor_of * one(*cut)
    return factor_of


def split_up(amount, total, limit, slope):
    loads = [(1 << 20) // math.isqrt(rank ** slope) + 1 for rank in range(2, amount + 1)]
    spare, holding = total - limit - (amount - 1), [1] * (amount - 1)
    while spare > 0:
        candidates = [i for i in range(amount - 1) if holding[i] < limit]
        whole, remaining = sum([loads[i] for i in candidates]), spare
        for i in candidates:
            addition = min(limit - holding[i], max(1, remaining * loads[i] // whole), spare)
            holding[i] = holding[i] + addition
            spare = spare - addition
    return np.array([limit] + holding)


def uneven(key, count, total, bound, skew):
    if count == 2:
        one = jax.random.randint(key, (), max(1, total - bound), min(bound, total - 1) + 1)
        return jnp.stack([one, total - one])
    sizes = jnp.asarray(split_up(count, total, bound, skew), jnp.int32)
    pairs = (count - 1) // 2
    source_of, taker = sizes[1:1 + 2 * pairs:2], sizes[2:2 + 2 * pairs:2]
    room = jnp.minimum(source_of - 1, bound - taker)
    passed = jax.random.randint(jax.random.fold_in(key, 1), (pairs,), 0, 1 << 20) % (room + 1)
    sizes = sizes.at[1:1 + 2 * pairs:2].set(source_of - passed).at[2:2 + 2 * pairs:2].set(taker + passed)
    return sizes[jax.random.permutation(jax.random.fold_in(key, 2), count)]


def noise(key, extent, deviation, limit, pieces=(), held_as=jnp.bfloat16):
    drawn = deviation * jax.random.normal(key, extent, jnp.float32)
    if pieces:
        drawn = drawn * block_levels(key, extent, pieces, -0.22, 0.18)
    return jnp.clip(drawn, -limit, limit).astype(held_as)


def setup_inputs(seed: int = 0, part: int = 0) -> dict:
    splits = jax.random.split(jax.random.key(seed), 7)
    own_keys = jax.random.split(jax.random.fold_in(splits[6], part), 7)
    return {
        "queries": draw_queries(jax.random.fold_in(jax.random.fold_in(splits[6], part), 71), part),
        "stored_key_rows": draw_stored_key_rows(jax.random.fold_in(jax.random.fold_in(splits[6], part), 71), part),
        "stored_value_rows": noise(own_keys[2], (TOKEN_LENGTH, KEY_VALUE_HEADS * HEAD_SIZE), 1.0, 6.0, ((0, 64),)),
        "grad_out": noise(own_keys[3], (TOKEN_LENGTH, QUERY_HEADS * HEAD_SIZE), 1.0, 6.0, ((0, 64),)),
        "segment_ids": jnp.searchsorted(jnp.cumsum(uneven(own_keys[4], DOCS, TOKEN_LENGTH, BLOCK // 2, 0)), jnp.arange(TOKEN_LENGTH), side="right").astype(jnp.int32),
        "stored_block_order": jax.random.permutation(own_keys[5], 2 * N_SEQ).astype(jnp.int32),
    }


def reference(queries, stored_key_rows, stored_value_rows, grad_out, segment_ids, stored_block_order):
    count_of_blocks = stored_block_order.shape[0]
    rows_per_block = BLOCK
    slots = jnp.arange(count_of_blocks, dtype=jnp.int32)
    match = stored_block_order[:, None] == slots[None, :]
    inverse_order = lax.optimization_barrier(jnp.sum(jnp.where(match, slots[:, None], 0), axis=0)).astype(jnp.int32)
    per_dev = QUERY_HEADS // N_HEAD
    query_group_size = QUERY_HEADS // KEY_VALUE_HEADS
    score_scale = 1.0 / math.sqrt(HEAD_SIZE)
    query_all = queries.reshape(count_of_blocks, rows_per_block, QUERY_HEADS, HEAD_SIZE)
    grad_all = grad_out.reshape(count_of_blocks, rows_per_block, QUERY_HEADS, HEAD_SIZE)
    sorted_key_rows = jnp.take(stored_key_rows.reshape(count_of_blocks, rows_per_block, KEY_VALUE_HEADS, HEAD_SIZE), inverse_order, axis=0)
    sorted_value_rows = jnp.take(stored_value_rows.reshape(count_of_blocks, rows_per_block, KEY_VALUE_HEADS, HEAD_SIZE), inverse_order, axis=0)
    documents = segment_ids.reshape(count_of_blocks, rows_per_block)
    attended = jnp.zeros((count_of_blocks, rows_per_block, QUERY_HEADS, HEAD_SIZE), jnp.bfloat16)
    grad_query = jnp.zeros((count_of_blocks, rows_per_block, QUERY_HEADS, HEAD_SIZE), jnp.bfloat16)
    key_value_total = jnp.zeros((count_of_blocks, rows_per_block, KEY_VALUE_HEADS, 2, HEAD_SIZE), jnp.float32)

    def device_step(index, carry):
        attended, grad_query, key_value_total = carry
        seq_rank = (index // N_HEAD).astype(jnp.int32)
        head_pos = (index % N_HEAD).astype(jnp.int32)
        kv_head = (head_pos * per_dev // query_group_size).astype(jnp.int32)
        keys_head = lax.dynamic_index_in_dim(sorted_key_rows, kv_head, 2, keepdims=False)
        values_head = lax.dynamic_index_in_dim(sorted_value_rows, kv_head, 2, keepdims=False)
        partial_sum = jnp.zeros((count_of_blocks, rows_per_block, 2, HEAD_SIZE), jnp.float32)
        for which_block in range(2):
            stored = (2 * seq_rank + which_block).astype(jnp.int32)
            query_block_id = lax.dynamic_index_in_dim(stored_block_order, stored, 0, keepdims=False)
            window = jnp.maximum(query_block_id - 1, 0).astype(jnp.int32)
            query_rows = lax.dynamic_index_in_dim(query_all, stored, 0, keepdims=False)
            grad_rows = lax.dynamic_index_in_dim(grad_all, stored, 0, keepdims=False)
            query_head = lax.dynamic_slice_in_dim(query_rows, head_pos * per_dev, per_dev, 1).astype(jnp.float32)
            grad_head = lax.dynamic_slice_in_dim(grad_rows, head_pos * per_dev, per_dev, 1).astype(jnp.float32)
            key_part = lax.dynamic_slice_in_dim(keys_head, window, 2, 0).reshape(2 * rows_per_block, HEAD_SIZE).astype(jnp.float32)
            value_part = lax.dynamic_slice_in_dim(values_head, window, 2, 0).reshape(2 * rows_per_block, HEAD_SIZE).astype(jnp.float32)
            query_pos = query_block_id * rows_per_block + jnp.arange(rows_per_block, dtype=jnp.int32)
            key_pos = window * rows_per_block + jnp.arange(2 * rows_per_block, dtype=jnp.int32)
            query_doc = lax.dynamic_index_in_dim(documents, query_block_id, 0, keepdims=False)
            key_doc = lax.dynamic_slice_in_dim(documents, window, 2, 0).reshape(2 * rows_per_block)
            usable = (key_pos[None, :] <= query_pos[:, None]) & (key_doc[None, :] == query_doc[:, None])
            scores = jnp.einsum('qhd,kd->hqk', query_head, key_part) * score_scale
            masked = jnp.where(usable[None], scores, -jnp.inf)
            row_max = lax.optimization_barrier(jnp.max(masked, axis=2))
            log_total = row_max + jnp.log(lax.optimization_barrier(jnp.sum(jnp.exp(masked - row_max[:, :, None]), axis=2)))
            weights = jnp.exp(jnp.where(usable[None], scores - log_total[:, :, None], -jnp.inf))
            weights16 = weights.astype(jnp.bfloat16)
            output = jnp.einsum('hqk,kd->qhd', weights16.astype(jnp.float32), value_part).astype(jnp.bfloat16)
            delta = jnp.einsum('qhd,qhd->hq', grad_head, output.astype(jnp.float32))
            dprob = jnp.einsum('qhd,kd->hqk', grad_head, value_part)
            dscore = (weights * (dprob - delta[:, :, None]) * score_scale).astype(jnp.bfloat16)
            grad_q = jnp.einsum('hqk,kd->qhd', dscore.astype(jnp.float32), key_part).astype(jnp.bfloat16)
            grad_k = jnp.einsum('hqk,qhd->kd', dscore.astype(jnp.float32), query_head)
            grad_v = jnp.einsum('hqk,qhd->kd', weights16.astype(jnp.float32), grad_head)
            out_rows = lax.dynamic_update_slice_in_dim(lax.dynamic_index_in_dim(attended, stored, 0, keepdims=False), output, head_pos * per_dev, 1)
            attended = lax.dynamic_update_index_in_dim(attended, out_rows, stored, 0)
            gq_rows = lax.dynamic_update_slice_in_dim(lax.dynamic_index_in_dim(grad_query, stored, 0, keepdims=False), grad_q, head_pos * per_dev, 1)
            grad_query = lax.dynamic_update_index_in_dim(grad_query, gq_rows, stored, 0)
            pair = jnp.stack([grad_k, grad_v], axis=1).reshape(2, rows_per_block, 2, HEAD_SIZE)
            previous = lax.dynamic_slice_in_dim(partial_sum, window, 2, 0)
            partial_sum = lax.dynamic_update_slice_in_dim(partial_sum, previous + pair, window, 0)
        rounded = lax.optimization_barrier(partial_sum.astype(jnp.bfloat16)).astype(jnp.float32)
        current = lax.dynamic_index_in_dim(key_value_total, kv_head, 2, keepdims=False)
        key_value_total = lax.dynamic_update_index_in_dim(key_value_total, current + rounded, kv_head, 2)
        return (attended, grad_query, key_value_total)
    attended, grad_query, key_value_total = lax.fori_loop(0, N_SEQ * N_HEAD, device_step, (attended, grad_query, key_value_total))
    key_value_stored = jnp.take(key_value_total, stored_block_order, axis=0).reshape(count_of_blocks * rows_per_block, KEY_VALUE_HEADS, 2, HEAD_SIZE)
    key_gradient = key_value_stored[:, :, 0].reshape(count_of_blocks * rows_per_block, KEY_VALUE_HEADS * HEAD_SIZE).astype(jnp.bfloat16)
    value_gradient = key_value_stored[:, :, 1].reshape(count_of_blocks * rows_per_block, KEY_VALUE_HEADS * HEAD_SIZE).astype(jnp.bfloat16)
    attended = attended.reshape(count_of_blocks * rows_per_block, QUERY_HEADS * HEAD_SIZE)
    grad_query = grad_query.reshape(count_of_blocks * rows_per_block, QUERY_HEADS * HEAD_SIZE)
    return (attended, grad_query, key_gradient, value_gradient)
```

```python
import functools
import math

import jax
import jax.numpy as jnp
from jax import lax
from jax.experimental import pallas as pl
from jax.experimental.pallas import tpu as pltpu
from jax.sharding import PartitionSpec as P

HEAD_SIZE = 128
QUERY_HEADS = 32
KEY_VALUE_HEADS = 4
GROUP = QUERY_HEADS // KEY_VALUE_HEADS
CHUNK = 128
WINDOW = 3 * CHUNK
KV_WIDTH = KEY_VALUE_HEADS * HEAD_SIZE
AXES = ("seq", "head")


def attend_kernel(
    info_ref,
    segments_ref,
    query_ref,
    grad_ref,
    key_far_ref,
    value_far_ref,
    key_near_ref,
    value_near_ref,
    key_own_ref,
    value_own_ref,
    out_ref,
    grad_query_ref,
    far_key_ref,
    far_value_ref,
    near_key_ref,
    near_value_ref,
    own_key_ref,
    own_value_ref,
    bias_ref,
):
    @pl.when(pl.program_id(0) == 0)
    def _():
        chunk = info_ref[0]
        own_row = segments_ref[pl.ds(chunk, 1), :]
        query_doc = jnp.broadcast_to(own_row, (CHUNK, CHUNK))
        for back in (2, 1, 0):
            at = chunk - back
            row = segments_ref[pl.ds(jnp.maximum(at, 0), 1), :]
            row = jnp.where(at >= 0, row, -1)
            key_doc = jnp.broadcast_to(row, (CHUNK, CHUNK)).T
            usable = key_doc == query_doc
            if back == 0:
                usable &= lax.broadcasted_iota(jnp.int32, (CHUNK, CHUNK), 0) <= (
                    lax.broadcasted_iota(jnp.int32, (CHUNK, CHUNK), 1)
                )
            tile = jnp.where(usable, 0.0, -jnp.inf).astype(jnp.float32)
            rows = pl.ds((2 - back) * CHUNK, CHUNK)
            bias_ref[rows, 0:CHUNK] = tile
            bias_ref[rows, CHUNK : 2 * CHUNK] = tile

    scale = 1.0 / math.sqrt(HEAD_SIZE)
    keys = jnp.concatenate([key_far_ref[...], key_near_ref[...], key_own_ref[...]], axis=0)
    values = jnp.concatenate([value_far_ref[...], value_near_ref[...], value_own_ref[...]], axis=0)
    keys_t = keys.T
    values_t = values.T
    last = (((1,), (1,)), ((), ()))
    plain = (((1,), (0,)), ((), ()))
    weight_parts, dscore_parts, query_parts, grad_parts = [], [], [], []
    for pair in range(GROUP // 2):
        heads = (2 * pair, 2 * pair + 1)
        queries = jnp.concatenate(
            [query_ref[:, a * HEAD_SIZE : (a + 1) * HEAD_SIZE] for a in heads], axis=0
        )
        grads = jnp.concatenate(
            [grad_ref[:, a * HEAD_SIZE : (a + 1) * HEAD_SIZE] for a in heads], axis=0
        )
        scores = lax.dot_general(keys, queries, last, preferred_element_type=jnp.float32)
        scores = scores + bias_ref[...]
        top = jnp.max(scores, axis=0, keepdims=True)
        raised = jnp.exp2((scores - top) * (scale * math.log2(math.e)))
        weights = raised * (1.0 / jnp.sum(raised, axis=0, keepdims=True))
        weights16 = weights.astype(jnp.bfloat16)
        dprob = lax.dot_general(values, grads, last, preferred_element_type=jnp.float32)
        product = weights * dprob
        delta = jnp.sum(product, axis=0, keepdims=True)
        dscore = ((product - weights * delta) * scale).astype(jnp.bfloat16)
        output_t = lax.dot_general(values_t, weights16, plain, preferred_element_type=jnp.float32)
        grad_query_t = lax.dot_general(keys_t, dscore, plain, preferred_element_type=jnp.float32)
        for i, a in enumerate(heads):
            columns = slice(a * HEAD_SIZE, (a + 1) * HEAD_SIZE)
            part = slice(i * CHUNK, (i + 1) * CHUNK)
            out_ref[:, columns] = output_t[:, part].T.astype(jnp.bfloat16)
            grad_query_ref[:, columns] = grad_query_t[:, part].T.astype(jnp.bfloat16)
        weight_parts.append(weights16)
        dscore_parts.append(dscore)
        query_parts.append(queries)
        grad_parts.append(grads)
    grad_keys = lax.dot_general(
        jnp.concatenate(dscore_parts, axis=1),
        jnp.concatenate(query_parts, axis=0),
        plain,
        preferred_element_type=jnp.float32,
    )
    grad_values = lax.dot_general(
        jnp.concatenate(weight_parts, axis=1),
        jnp.concatenate(grad_parts, axis=0),
        plain,
        preferred_element_type=jnp.float32,
    )
    far_key_ref[...] = grad_keys[:CHUNK].astype(jnp.bfloat16)
    near_key_ref[...] = grad_keys[CHUNK : 2 * CHUNK].astype(jnp.bfloat16)
    own_key_ref[...] = grad_keys[2 * CHUNK :]
    far_value_ref[...] = grad_values[:CHUNK].astype(jnp.bfloat16)
    near_value_ref[...] = grad_values[CHUNK : 2 * CHUNK].astype(jnp.bfloat16)
    own_value_ref[...] = grad_values[2 * CHUNK :]


def attend(chunk, segments, queries, grads, far, near, own):
    rows = queries.shape[0]
    wide = pl.BlockSpec((rows, GROUP * HEAD_SIZE), lambda g, info: (0, g))
    narrow = pl.BlockSpec((rows, HEAD_SIZE), lambda g, info: (0, g))
    half = jax.ShapeDtypeStruct((rows, KV_WIDTH), jnp.bfloat16)
    full = jax.ShapeDtypeStruct((rows, KV_WIDTH), jnp.float32)
    products = 6 * 2 * rows * QUERY_HEADS * WINDOW * HEAD_SIZE
    return pl.pallas_call(
        attend_kernel,
        grid_spec=pltpu.PrefetchScalarGridSpec(
            num_scalar_prefetch=1,
            grid=(KEY_VALUE_HEADS,),
            in_specs=[
                pl.BlockSpec(segments.shape, lambda g, info: (0, 0)),
                wide,
                wide,
                narrow,
                narrow,
                narrow,
                narrow,
                narrow,
                narrow,
            ],
            out_specs=[wide, wide] + [narrow] * 6,
            scratch_shapes=[pltpu.VMEM((WINDOW, 2 * CHUNK), jnp.float32)],
        ),
        out_shape=[
            jax.ShapeDtypeStruct(queries.shape, jnp.bfloat16),
            jax.ShapeDtypeStruct(queries.shape, jnp.bfloat16),
            half,
            half,
            half,
            half,
            full,
            full,
        ],
        compiler_params=pltpu.CompilerParams(vmem_limit_bytes=48 * 1024 * 1024),
        cost_estimate=pl.CostEstimate(
            flops=products,
            bytes_accessed=8 * rows * QUERY_HEADS * HEAD_SIZE,
            transcendentals=rows * QUERY_HEADS * WINDOW,
        ),
    )(chunk, segments, queries, grads, *far, *near, *own)


def within_block(moves):
    return [
        (s * 8 + b * 4 + source, s * 8 + b * 4 + target)
        for s in range(8)
        for b in range(2)
        for source, target in moves
    ]


def to_seq(value, mask):
    if mask == 0:
        return value
    return lax.ppermute(value, "seq", [(s, s ^ mask) for s in range(8)])


def to_plane(value, mask):
    if mask == 0:
        return value
    return lax.ppermute(
        value,
        AXES,
        [(s * 8 + h, (s ^ (mask >> 1)) * 8 + (h ^ ((mask & 1) * 4))) for s in range(8) for h in range(8)],
    )


def pick(stack, index):
    return lax.dynamic_index_in_dim(stack, index, 0, keepdims=False)


def local(queries, keys, values, grads, segment_ids, order):
    s = lax.axis_index("seq")
    h = lax.axis_index("head")
    z, y = s // 4, s % 4
    block, c = h // 4, h % 4
    count = order.shape[0]
    slots = jnp.arange(count, dtype=jnp.int32)
    step = order[:, None] - order[None, :]
    before = jnp.sum(jnp.where((step == 1) | (step == 1 - count), slots[None, :], 0), axis=1)
    after = jnp.sum(jnp.where((step == -1) | (step == count - 1), slots[None, :], 0), axis=1)
    mine = 2 * s + block
    before_mine = pick(before, mine)
    after_mine = pick(after, mine)

    near_in = [lax.ppermute(t, AXES, within_block([(0, 1), (1, 2), (2, 3)])) for t in (keys, values)]
    far_in = [lax.ppermute(t, AXES, within_block([(0, 2), (1, 3)])) for t in (keys, values)]

    moved = lax.ppermute(values, AXES, within_block([(2, 0), (3, 1)]))
    quarter = jnp.where(c >= 2, keys, moved).reshape(4, CHUNK // 4, KV_WIDTH)
    pieces = [pick(quarter, y ^ m) for m in range(4)]
    held = jnp.stack([to_seq(pieces[m % 4], m) for m in range(8)], axis=0)
    arrived = []
    for mask in range(8):
        target = 2 * (s ^ (mask >> 1)) + (block ^ (mask & 1))
        arrived.append(to_plane(pick(held, (pick(before, target) >> 1) ^ s), mask))
    arrived = jnp.stack(arrived, axis=0).reshape(4, 2, CHUNK // 4, KV_WIDTH)
    arrived = lax.dynamic_index_in_dim(arrived, (before_mine & 1) ^ block, 1, keepdims=False)
    quarter = jnp.concatenate([pick(arrived, m ^ y) for m in range(4)], axis=0)
    straight = lax.ppermute(quarter, AXES, within_block([(2, 0), (3, 1)]))
    to_first = lax.ppermute(quarter, AXES, within_block([(1, 0)]))
    across = lax.ppermute(quarter, AXES, within_block([(3, 0)]))
    far = (jnp.where(c < 2, straight, far_in[0]), jnp.where(c < 2, quarter, far_in[1]))
    near = (jnp.where(c == 0, across, near_in[0]), jnp.where(c == 0, to_first, near_in[1]))

    chunk = (pick(order, mine) * 4 + c).reshape(1)
    attended, grad_query, far_key, far_value, near_key, near_value, own_key, own_value = attend(
        chunk, segment_ids.reshape(-1, CHUNK), queries, grads, far, near, (keys, values)
    )

    straight = lax.ppermute(far_key, AXES, within_block([(0, 2), (1, 3)]))
    to_second = lax.ppermute(near_value, AXES, within_block([(0, 1)]))
    across = lax.ppermute(near_key, AXES, within_block([(0, 3)]))
    near_back = [
        lax.ppermute(t, AXES, within_block([(1, 0), (2, 1), (3, 2)])) for t in (near_key, near_value)
    ]
    far_back = [lax.ppermute(t, AXES, within_block([(2, 0), (3, 1)])) for t in (far_key, far_value)]
    quarter = jnp.where(c < 2, far_value, straight).astype(jnp.float32)
    quarter = quarter + jnp.where(c == 1, to_second, jnp.where(c == 3, across, 0)).astype(jnp.float32)
    quarter = quarter.astype(jnp.bfloat16).reshape(4, CHUNK // 4, KV_WIDTH)
    pieces = [pick(quarter, y ^ m) for m in range(4)]
    held = jnp.stack([to_plane(pieces[mask >> 1], mask) for mask in range(8)], axis=0)
    arrived = []
    for m in range(8):
        target = pick(after, 2 * (s ^ m) + block)
        index = ((((target >> 1) ^ s) & 3) << 1) | ((target & 1) ^ block)
        arrived.append(to_seq(pick(held, index), m))
    arrived = jnp.stack(arrived, axis=0).reshape(2, 4, CHUNK // 4, KV_WIDTH)
    arrived = pick(arrived, (after_mine >> 3) ^ z)
    quarter = jnp.concatenate([pick(arrived, m ^ y) for m in range(4)], axis=0)
    moved = lax.ppermute(quarter, AXES, within_block([(0, 2), (1, 3)]))

    wide = functools.partial(jnp.asarray, dtype=jnp.float32)
    key_gradient = own_key + wide(near_back[0]) + wide(far_back[0]) + wide(jnp.where(c >= 2, quarter, 0))
    value_gradient = own_value + wide(near_back[1]) + wide(far_back[1]) + wide(jnp.where(c >= 2, moved, 0))
    return (
        attended,
        grad_query,
        key_gradient.astype(jnp.bfloat16),
        value_gradient.astype(jnp.bfloat16),
    )


def solution(mesh):
    rows = P(("dp", "seq", "head"), None)
    return jax.shard_map(
        local,
        mesh=mesh,
        in_specs=(rows, rows, rows, rows, P("dp"), P("dp")),
        out_specs=(rows, rows, rows, rows),
        check_vma=False,
    )
```

```python
import math

import jax
import jax.numpy as jnp
from jax import lax
from jax.experimental import pallas as pl
from jax.experimental.pallas import tpu as pltpu
from jax.sharding import PartitionSpec as P

HEAD_SIZE = 128
QUERY_HEADS = 32
KEY_VALUE_HEADS = 4
GROUP = QUERY_HEADS // KEY_VALUE_HEADS
CHUNK = 128
WINDOW = 3 * CHUNK
KV_WIDTH = KEY_VALUE_HEADS * HEAD_SIZE
BLOCK_AXES = ("x", "core")
SEQ_AXES = ("z", "y")
PLANE_AXES = ("y", "b")


def attend_kernel(
    info_ref,
    segments_ref,
    query_ref,
    grad_ref,
    far_ref,
    near_ref,
    own_ref,
    out_ref,
    grad_query_ref,
    far_grad_ref,
    near_grad_ref,
    own_grad_ref,
    bias_ref,
):
    @pl.when(pl.program_id(0) == 0)
    def _():
        chunk = info_ref[0]
        own_row = segments_ref[pl.ds(chunk, 1), :]
        query_doc = jnp.broadcast_to(own_row, (CHUNK, CHUNK))
        for back in (2, 1, 0):
            at = chunk - back
            row = segments_ref[pl.ds(jnp.maximum(at, 0), 1), :]
            row = jnp.where(at >= 0, row, -1)
            key_doc = jnp.broadcast_to(row, (CHUNK, CHUNK)).T
            usable = key_doc == query_doc
            if back == 0:
                usable &= lax.broadcasted_iota(jnp.int32, (CHUNK, CHUNK), 0) <= (
                    lax.broadcasted_iota(jnp.int32, (CHUNK, CHUNK), 1)
                )
            tile = jnp.where(usable, 0.0, -jnp.inf).astype(jnp.float32)
            rows = pl.ds((2 - back) * CHUNK, CHUNK)
            bias_ref[rows, 0:CHUNK] = tile
            bias_ref[rows, CHUNK : 2 * CHUNK] = tile

    scale = 1.0 / math.sqrt(HEAD_SIZE)
    keys = jnp.concatenate([far_ref[0], near_ref[0], own_ref[0]], axis=0)
    values = jnp.concatenate([far_ref[1], near_ref[1], own_ref[1]], axis=0)
    keys_t = keys.T
    values_t = values.T
    last = (((1,), (1,)), ((), ()))
    plain = (((1,), (0,)), ((), ()))
    weight_parts, dscore_parts, query_parts, grad_parts = [], [], [], []
    for pair in range(GROUP // 2):
        heads = (2 * pair, 2 * pair + 1)
        queries = jnp.concatenate(
            [query_ref[:, a * HEAD_SIZE : (a + 1) * HEAD_SIZE] for a in heads], axis=0
        )
        grads = jnp.concatenate(
            [grad_ref[:, a * HEAD_SIZE : (a + 1) * HEAD_SIZE] for a in heads], axis=0
        )
        scores = lax.dot_general(keys, queries, last, preferred_element_type=jnp.float32)
        scores = scores + bias_ref[...]
        top = jnp.max(scores, axis=0, keepdims=True)
        raised = jnp.exp2((scores - top) * (scale * math.log2(math.e)))
        weights = raised * (1.0 / jnp.sum(raised, axis=0, keepdims=True))
        weights16 = weights.astype(jnp.bfloat16)
        dprob = lax.dot_general(values, grads, last, preferred_element_type=jnp.float32)
        product = weights * dprob
        delta = jnp.sum(product, axis=0, keepdims=True)
        dscore = ((product - weights * delta) * scale).astype(jnp.bfloat16)
        output_t = lax.dot_general(values_t, weights16, plain, preferred_element_type=jnp.float32)
        grad_query_t = lax.dot_general(keys_t, dscore, plain, preferred_element_type=jnp.float32)
        for i, a in enumerate(heads):
            columns = slice(a * HEAD_SIZE, (a + 1) * HEAD_SIZE)
            part = slice(i * CHUNK, (i + 1) * CHUNK)
            out_ref[:, columns] = output_t[:, part].astype(jnp.bfloat16).T
            grad_query_ref[:, columns] = grad_query_t[:, part].astype(jnp.bfloat16).T
        weight_parts.append(weights16)
        dscore_parts.append(dscore)
        query_parts.append(queries)
        grad_parts.append(grads)
    grad_keys = lax.dot_general(
        jnp.concatenate(dscore_parts, axis=1),
        jnp.concatenate(query_parts, axis=0),
        plain,
        preferred_element_type=jnp.float32,
    )
    grad_values = lax.dot_general(
        jnp.concatenate(weight_parts, axis=1),
        jnp.concatenate(grad_parts, axis=0),
        plain,
        preferred_element_type=jnp.float32,
    )
    for i, total in enumerate((grad_keys, grad_values)):
        far_grad_ref[i] = total[:CHUNK].astype(jnp.bfloat16)
        near_grad_ref[i] = total[CHUNK : 2 * CHUNK].astype(jnp.bfloat16)
        own_grad_ref[i] = total[2 * CHUNK :]


def attend(chunk, segments, queries, grads, far, near, own):
    rows = queries.shape[0]
    wide = pl.BlockSpec((rows, GROUP * HEAD_SIZE), lambda g, info: (0, g))
    pair = pl.BlockSpec((2, rows, HEAD_SIZE), lambda g, info: (0, 0, g))
    half = jax.ShapeDtypeStruct((2, rows, KV_WIDTH), jnp.bfloat16)
    full = jax.ShapeDtypeStruct((2, rows, KV_WIDTH), jnp.float32)
    return pl.pallas_call(
        attend_kernel,
        grid_spec=pltpu.PrefetchScalarGridSpec(
            num_scalar_prefetch=1,
            grid=(KEY_VALUE_HEADS,),
            in_specs=[
                pl.BlockSpec(segments.shape, lambda g, info: (0, 0)),
                wide,
                wide,
                pair,
                pair,
                pair,
            ],
            out_specs=[wide, wide, pair, pair, pair],
            scratch_shapes=[pltpu.VMEM((WINDOW, 2 * CHUNK), jnp.float32)],
        ),
        out_shape=[
            jax.ShapeDtypeStruct(queries.shape, jnp.bfloat16),
            jax.ShapeDtypeStruct(queries.shape, jnp.bfloat16),
            half,
            half,
            full,
        ],
        compiler_params=pltpu.CompilerParams(vmem_limit_bytes=48 * 1024 * 1024),
        cost_estimate=pl.CostEstimate(
            flops=6 * 2 * rows * QUERY_HEADS * WINDOW * HEAD_SIZE,
            bytes_accessed=8 * rows * QUERY_HEADS * HEAD_SIZE,
            transcendentals=rows * QUERY_HEADS * WINDOW,
        ),
    )(chunk, segments, queries, grads, far, near, own)


def move(value, moves):
    return lax.ppermute(value, BLOCK_AXES, moves)


def exchange(pieces, axes):
    return lax.all_to_all(pieces, axes, 0, 0)


def pick(stack, index):
    return lax.dynamic_index_in_dim(stack, index, 0, keepdims=False)


def local(queries, keys, values, grads, segment_ids, order):
    s = lax.axis_index(SEQ_AXES)
    z = lax.axis_index("z")
    block = lax.axis_index("b")
    c = lax.axis_index(BLOCK_AXES)
    count = order.shape[0]
    slots = jnp.arange(count, dtype=jnp.int32)
    step = order[:, None] - order[None, :]
    before = jnp.sum(jnp.where((step == 1) | (step == 1 - count), slots[None, :], 0), axis=1)
    after = jnp.sum(jnp.where((step == -1) | (step == count - 1), slots[None, :], 0), axis=1)
    mine = 2 * s + block
    part = (4, CHUNK // 4, KV_WIDTH)

    moved = move(values, [(2, 0), (3, 1)])
    own = jnp.stack([keys, values], axis=0)
    near_in = move(own, [(0, 1), (1, 2), (2, 3)])
    far_in = move(own, [(0, 2), (1, 3)])
    quarter = jnp.where(c >= 2, keys, moved).reshape(part)
    held = exchange(jnp.concatenate([quarter, quarter], axis=0), SEQ_AXES)
    sources = lax.dynamic_slice_in_dim(before, 8 * z, 8) >> 1
    arrived = exchange(jnp.stack([pick(held, sources[i]) for i in range(8)], axis=0), PLANE_AXES)
    arrived = arrived.reshape(4, 2, *part[1:])
    quarter = lax.dynamic_index_in_dim(arrived, pick(before, mine) & 1, 1, keepdims=False)
    quarter = quarter.reshape(CHUNK, KV_WIDTH)
    straight = move(quarter, [(2, 0), (3, 1)])
    to_first = move(quarter, [(1, 0)])
    across = move(quarter, [(3, 0)])
    far = jnp.where(c < 2, jnp.stack([straight, quarter], axis=0), far_in)
    near = jnp.where(c == 0, jnp.stack([across, to_first], axis=0), near_in)

    chunk = (pick(order, mine) * 4 + c).reshape(1)
    attended, grad_query, far_grad, near_grad, own_grad = attend(
        chunk, segment_ids.reshape(-1, CHUNK), queries, grads, far, near, own
    )

    straight = move(far_grad[0], [(0, 2), (1, 3)])
    to_second = move(near_grad[1], [(0, 1)])
    across = move(near_grad[0], [(0, 3)])
    near_back = move(near_grad, [(1, 0), (2, 1), (3, 2)])
    far_back = move(far_grad, [(2, 0), (3, 1)])
    quarter = jnp.where(c < 2, far_grad[1], straight).astype(jnp.float32)
    quarter = quarter + jnp.where(c == 1, to_second, jnp.where(c == 3, across, 0)).astype(jnp.float32)
    quarter = quarter.astype(jnp.bfloat16).reshape(part)
    held = exchange(jnp.repeat(quarter, 2, axis=0), PLANE_AXES)
    targets = lax.dynamic_slice_in_dim(after.reshape(8, 2), block, 1, 1)[:, 0] & 7
    arrived = exchange(jnp.stack([pick(held, targets[i]) for i in range(8)], axis=0), SEQ_AXES)
    quarter = pick(arrived.reshape(2, *part), pick(after, mine) >> 3).reshape(CHUNK, KV_WIDTH)
    moved = move(quarter, [(0, 2), (1, 3)])

    total = own_grad + near_back.astype(jnp.float32) + far_back.astype(jnp.float32)
    late = jnp.where(c >= 2, jnp.stack([quarter, moved], axis=0), 0)
    total = (total + late.astype(jnp.float32)).astype(jnp.bfloat16)
    return attended, grad_query, total[0], total[1]


def solution(mesh):
    names = ("dp", "z", "y", "b", "x", "core")
    fine = jax.sharding.Mesh(mesh.devices.reshape(-1, 2, 4, 2, 2, 2), names)
    rows = P(names, None)
    return jax.shard_map(
        local,
        mesh=fine,
        in_specs=(rows, rows, rows, rows, P("dp"), P("dp")),
        out_specs=(rows, rows, rows, rows),
        check_vma=False,
    )
```

```python
import functools
import math

import jax
import jax.numpy as jnp
from jax import lax
from jax.experimental import pallas as pl
from jax.experimental.pallas import tpu as pltpu
from jax.sharding import PartitionSpec as P

HEAD_SIZE = 128
QUERY_HEADS = 32
KEY_VALUE_HEADS = 4
GROUP = QUERY_HEADS // KEY_VALUE_HEADS
CHUNK = 128
WINDOW = 3 * CHUNK
KV_WIDTH = KEY_VALUE_HEADS * HEAD_SIZE
BLOCK_AXES = ("x", "core")
SEQ_AXES = ("z", "y")
PLANE_AXES = ("y", "b")


def usable_bias(chunk, segments_ref, bias_ref):
    query_doc = jnp.broadcast_to(segments_ref[pl.ds(chunk, 1), :], (CHUNK, CHUNK))
    for back in (2, 1, 0):
        at = chunk - back
        row = segments_ref[pl.ds(jnp.maximum(at, 0), 1), :]
        row = jnp.where(at >= 0, row, -1)
        usable = jnp.broadcast_to(row, (CHUNK, CHUNK)).T == query_doc
        if back == 0:
            usable &= lax.broadcasted_iota(jnp.int32, (CHUNK, CHUNK), 0) <= (
                lax.broadcasted_iota(jnp.int32, (CHUNK, CHUNK), 1)
            )
        tile = jnp.where(usable, 0.0, -jnp.inf).astype(jnp.float32)
        rows = pl.ds((2 - back) * CHUNK, CHUNK)
        bias_ref[rows, 0:CHUNK] = tile
        bias_ref[rows, CHUNK : 2 * CHUNK] = tile


def stacked(ref, heads):
    return jnp.concatenate(
        [ref[:, a * HEAD_SIZE : (a + 1) * HEAD_SIZE] for a in heads], axis=0
    )


LAST = (((1,), (1,)), ((), ()))
PLAIN = (((1,), (0,)), ((), ()))


def dot(left, right, dims):
    return lax.dot_general(left, right, dims, preferred_element_type=jnp.float32)


def score_kernel(
    order_ref,
    place_ref,
    segments_ref,
    query_ref,
    grad_ref,
    far_ref,
    near_ref,
    own_ref,
    weight_ref,
    dscore_ref,
    far_grad_ref,
    near_grad_ref,
    bias_ref,
):
    @pl.when(pl.program_id(0) == 0)
    def _():
        usable_bias(order_ref[place_ref[2]] * 4 + place_ref[3], segments_ref, bias_ref)

    scale = 1.0 / math.sqrt(HEAD_SIZE)
    keys = jnp.concatenate([far_ref[0], near_ref[0], own_ref[0]], axis=0)
    values = jnp.concatenate([far_ref[1], near_ref[1], own_ref[1]], axis=0)
    width = 2 * CHUNK
    for pair in range(GROUP // 2):
        heads = (2 * pair, 2 * pair + 1)
        scores = dot(keys, stacked(query_ref, heads), LAST) + bias_ref[...]
        top = jnp.max(scores, axis=0, keepdims=True)
        raised = jnp.exp2((scores - top) * (scale * math.log2(math.e)))
        weights = raised * (1.0 / jnp.sum(raised, axis=0, keepdims=True))
        product = weights * dot(values, stacked(grad_ref, heads), LAST)
        delta = jnp.sum(product, axis=0, keepdims=True)
        columns = pl.ds(pair * width, width)
        weight_ref[:, columns] = weights.astype(jnp.bfloat16)
        dscore_ref[:, columns] = ((product - weights * delta) * scale).astype(jnp.bfloat16)
    every = range(GROUP)
    halo = pl.ds(0, 2 * CHUNK)
    grad_keys = dot(dscore_ref[halo, :], stacked(query_ref, every), PLAIN).astype(jnp.bfloat16)
    grad_values = dot(weight_ref[halo, :], stacked(grad_ref, every), PLAIN).astype(jnp.bfloat16)
    for i, total in enumerate((grad_keys, grad_values)):
        far_grad_ref[i] = total[:CHUNK]
        near_grad_ref[i] = total[CHUNK:]


def output_kernel(
    query_ref,
    grad_ref,
    far_ref,
    near_ref,
    own_ref,
    weight_ref,
    dscore_ref,
    out_ref,
    grad_query_ref,
    own_grad_ref,
):
    keys_t = jnp.concatenate([far_ref[0], near_ref[0], own_ref[0]], axis=0).T
    values_t = jnp.concatenate([far_ref[1], near_ref[1], own_ref[1]], axis=0).T
    width = 2 * CHUNK
    for pair in range(GROUP // 2):
        columns = pl.ds(pair * width, width)
        output_t = dot(values_t, weight_ref[:, columns], PLAIN).astype(jnp.bfloat16)
        grad_query_t = dot(keys_t, dscore_ref[:, columns], PLAIN).astype(jnp.bfloat16)
        for i in range(2):
            columns = pl.ds(pair * width + i * CHUNK, CHUNK)
            part = slice(i * CHUNK, (i + 1) * CHUNK)
            out_ref[:, columns] = output_t[:, part].T
            grad_query_ref[:, columns] = grad_query_t[:, part].T
    every = range(GROUP)
    own = pl.ds(2 * CHUNK, CHUNK)
    own_grad_ref[0] = dot(dscore_ref[own, :], stacked(query_ref, every), PLAIN)
    own_grad_ref[1] = dot(weight_ref[own, :], stacked(grad_ref, every), PLAIN)


def attention_specs(rows):
    wide = pl.BlockSpec((rows, GROUP * HEAD_SIZE), lambda g, *_: (0, g))
    pair = pl.BlockSpec((2, rows, HEAD_SIZE), lambda g, *_: (0, 0, g))
    window = pl.BlockSpec((WINDOW, GROUP * HEAD_SIZE), lambda g, *_: (0, g))
    return wide, pair, window


def scores_and_halo(order, place, segments, queries, grads, far, near, own):
    rows = queries.shape[0]
    wide, pair, window = attention_specs(rows)
    held = jax.ShapeDtypeStruct((WINDOW, queries.shape[1]), jnp.bfloat16)
    half = jax.ShapeDtypeStruct((2, rows, KV_WIDTH), jnp.bfloat16)
    return pl.pallas_call(
        score_kernel,
        grid_spec=pltpu.PrefetchScalarGridSpec(
            num_scalar_prefetch=2,
            grid=(KEY_VALUE_HEADS,),
            in_specs=[pl.BlockSpec(segments.shape, lambda g, *_: (0, 0)), wide, wide, pair, pair, pair],
            out_specs=[window, window, pair, pair],
            scratch_shapes=[pltpu.VMEM((WINDOW, 2 * CHUNK), jnp.float32)],
        ),
        out_shape=[held, held, half, half],
        compiler_params=pltpu.CompilerParams(vmem_limit_bytes=32 * 1024 * 1024),
        cost_estimate=pl.CostEstimate(
            flops=7 * rows * QUERY_HEADS * WINDOW * HEAD_SIZE,
            bytes_accessed=16 * rows * QUERY_HEADS * HEAD_SIZE,
            transcendentals=rows * QUERY_HEADS * WINDOW,
        ),
    )(order, place, segments, queries, grads, far, near, own)


def outputs_and_own(queries, grads, far, near, own, weights, dscores):
    rows = queries.shape[0]
    wide, pair, window = attention_specs(rows)
    like = jax.ShapeDtypeStruct(queries.shape, jnp.bfloat16)
    return pl.pallas_call(
        output_kernel,
        grid=(KEY_VALUE_HEADS,),
        in_specs=[wide, wide, pair, pair, pair, window, window],
        out_specs=[wide, wide, pair],
        out_shape=[like, like, jax.ShapeDtypeStruct((2, rows, KV_WIDTH), jnp.float32)],
        compiler_params=pltpu.CompilerParams(vmem_limit_bytes=32 * 1024 * 1024),
        cost_estimate=pl.CostEstimate(
            flops=5 * rows * QUERY_HEADS * WINDOW * HEAD_SIZE,
            bytes_accessed=20 * rows * QUERY_HEADS * HEAD_SIZE,
            transcendentals=0,
        ),
    )(queries, grads, far, near, own, weights, dscores)


def route_kernel(forward, order_ref, place_ref, held_ref, out_ref, slot_ref):
    count = order_ref.shape[0]
    for j in range(count):
        slot_ref[order_ref[j]] = j
    z, block = place_ref[0], place_ref[1]
    for i in range(8):
        if forward:
            other = slot_ref[lax.rem(order_ref[8 * z + i] + count - 1, count)]
            index, mine = lax.div(other, 2), lax.rem(other, 2) == block
        else:
            other = slot_ref[lax.rem(order_ref[2 * i + block] + 1, count)]
            index, mine = lax.rem(other, 8), lax.div(other, 8) == z

        @pl.when(mine)
        def _(i=i, index=index):
            out_ref[i] = held_ref[index]

        @pl.when(jnp.logical_not(mine))
        def _(i=i):
            out_ref[i] = jnp.zeros(out_ref.shape[1:], out_ref.dtype)


def route(order, place, held, forward):
    whole = pl.BlockSpec(held.shape, lambda i, *_: (0, 0, 0))
    return pl.pallas_call(
        functools.partial(route_kernel, forward),
        grid_spec=pltpu.PrefetchScalarGridSpec(
            num_scalar_prefetch=2,
            grid=(1,),
            in_specs=[whole],
            out_specs=whole,
            scratch_shapes=[pltpu.SMEM((order.shape[0],), jnp.int32)],
        ),
        out_shape=jax.ShapeDtypeStruct(held.shape, held.dtype),
        cost_estimate=pl.CostEstimate(flops=0, bytes_accessed=4 * held.size, transcendentals=0),
    )(order, place, held)


def move(value, moves):
    return lax.ppermute(value, BLOCK_AXES, moves)


def exchange(pieces, axes):
    return lax.all_to_all(pieces, axes, 0, 0)


def local(queries, keys, values, grads, segment_ids, order):
    z = lax.axis_index("z")
    block = lax.axis_index("b")
    c = lax.axis_index(BLOCK_AXES)
    place = jnp.stack([z, block, 8 * z + 2 * lax.axis_index("y") + block, c]).astype(jnp.int32)
    part = (4, CHUNK // 4, KV_WIDTH)
    whole = (CHUNK, KV_WIDTH)

    moved = move(values, [(2, 0), (3, 1)])
    own = jnp.stack([keys, values], axis=0)
    near_in = move(own, [(0, 1), (1, 2), (2, 3)])
    far_in = move(own, [(0, 2), (1, 3)])
    quarter = jnp.where(c >= 2, keys, moved).reshape(part)
    held = exchange(jnp.concatenate([quarter, quarter], axis=0), SEQ_AXES)
    held, near_in, far_in = lax.optimization_barrier((held, near_in, far_in))
    arrived = exchange(route(order, place, held, True), PLANE_AXES).reshape(4, 2, *part[1:])
    quarter = (arrived[:, 0] + arrived[:, 1]).reshape(whole)
    straight = move(quarter, [(2, 0), (3, 1)])
    to_first = move(quarter, [(1, 0)])
    across = move(quarter, [(3, 0)])
    far = jnp.where(c < 2, jnp.stack([straight, quarter], axis=0), far_in)
    near = jnp.where(c == 0, jnp.stack([across, to_first], axis=0), near_in)

    weights, dscores, far_grad, near_grad = scores_and_halo(
        order, place, segment_ids.reshape(-1, CHUNK), queries, grads, far, near, own
    )

    straight = move(far_grad[0], [(0, 2), (1, 3)])
    to_second = move(near_grad[1], [(0, 1)])
    across = move(near_grad[0], [(0, 3)])
    quarter = jnp.where(c < 2, far_grad[1], straight).astype(jnp.float32)
    quarter = quarter + jnp.where(c == 1, to_second, jnp.where(c == 3, across, 0)).astype(jnp.float32)
    quarter = quarter.astype(jnp.bfloat16).reshape(part)
    pieces = jnp.repeat(quarter, 2, axis=0)
    pieces, weights, dscores = lax.optimization_barrier((pieces, weights, dscores))
    held = exchange(pieces, PLANE_AXES)
    attended, grad_query, own_grad = outputs_and_own(queries, grads, far, near, own, weights, dscores)
    near_back = move(near_grad, [(1, 0), (2, 1), (3, 2)])
    far_back = move(far_grad, [(2, 0), (3, 1)])
    arrived = exchange(route(order, place, held, False), SEQ_AXES).reshape(2, *part)
    quarter = (arrived[0] + arrived[1]).reshape(whole)
    moved = move(quarter, [(0, 2), (1, 3)])

    total = own_grad + near_back.astype(jnp.float32) + far_back.astype(jnp.float32)
    key_gradient = total[0] + jnp.where(c >= 2, quarter, 0).astype(jnp.float32)
    value_gradient = total[1] + moved.astype(jnp.float32)
    return (
        attended,
        grad_query,
        key_gradient.astype(jnp.bfloat16),
        value_gradient.astype(jnp.bfloat16),
    )


def solution(mesh):
    names = ("dp", "z", "y", "b", "x", "core")
    fine = jax.sharding.Mesh(mesh.devices.reshape(-1, 2, 4, 2, 2, 2), names)
    rows = P(names, None)
    return jax.shard_map(
        local,
        mesh=fine,
        in_specs=(rows, rows, rows, rows, P("dp"), P("dp")),
        out_specs=(rows, rows, rows, rows),
        check_vma=False,
    )
```

```python
import functools
import math

import jax
import jax.numpy as jnp
from jax import lax
from jax.experimental import pallas as pl
from jax.experimental.pallas import tpu as pltpu
from jax.sharding import PartitionSpec as P

HEAD_SIZE = 128
QUERY_HEADS = 32
KEY_VALUE_HEADS = 4
GROUP = QUERY_HEADS // KEY_VALUE_HEADS
CHUNK = 128
WINDOW = 3 * CHUNK
KV_WIDTH = KEY_VALUE_HEADS * HEAD_SIZE
BLOCK_AXES = ("x", "core")
SEQ_AXES = ("z", "y")
PLANE_AXES = ("y", "b", "x")


def usable_bias(chunk, segments_ref, bias_ref):
    query_doc = jnp.broadcast_to(segments_ref[pl.ds(chunk, 1), :], (CHUNK, CHUNK))
    for back in (2, 1, 0):
        at = chunk - back
        row = segments_ref[pl.ds(jnp.maximum(at, 0), 1), :]
        row = jnp.where(at >= 0, row, -1)
        usable = jnp.broadcast_to(row, (CHUNK, CHUNK)).T == query_doc
        if back == 0:
            usable &= lax.broadcasted_iota(jnp.int32, (CHUNK, CHUNK), 0) <= (
                lax.broadcasted_iota(jnp.int32, (CHUNK, CHUNK), 1)
            )
        tile = jnp.where(usable, 0.0, -jnp.inf).astype(jnp.float32)
        rows = pl.ds((2 - back) * CHUNK, CHUNK)
        bias_ref[rows, 0:CHUNK] = tile
        bias_ref[rows, CHUNK : 2 * CHUNK] = tile


def stacked(ref, heads):
    return jnp.concatenate(
        [ref[:, a * HEAD_SIZE : (a + 1) * HEAD_SIZE] for a in heads], axis=0
    )


LAST = (((1,), (1,)), ((), ()))
PLAIN = (((1,), (0,)), ((), ()))


def dot(left, right, dims):
    return lax.dot_general(left, right, dims, preferred_element_type=jnp.float32)


def score_kernel(
    order_ref,
    place_ref,
    segments_ref,
    query_ref,
    grad_ref,
    far_ref,
    near_ref,
    own_ref,
    weight_ref,
    dscore_ref,
    far_grad_ref,
    near_grad_ref,
    bias_ref,
):
    @pl.when(pl.program_id(0) == 0)
    def _():
        usable_bias(order_ref[place_ref[2]] * 4 + place_ref[3], segments_ref, bias_ref)

    scale = 1.0 / math.sqrt(HEAD_SIZE)
    values = jnp.concatenate([far_ref[0], near_ref[0], own_ref[0]], axis=0)
    keys = jnp.concatenate([far_ref[1], near_ref[1], own_ref[1]], axis=0)
    width = 2 * CHUNK
    for pair in range(GROUP // 2):
        heads = (2 * pair, 2 * pair + 1)
        scores = dot(keys, stacked(query_ref, heads), LAST) + bias_ref[...]
        top = jnp.max(scores, axis=0, keepdims=True)
        raised = jnp.exp2((scores - top) * (scale * math.log2(math.e)))
        weights = raised * (1.0 / jnp.sum(raised, axis=0, keepdims=True))
        product = weights * dot(values, stacked(grad_ref, heads), LAST)
        delta = jnp.sum(product, axis=0, keepdims=True)
        columns = pl.ds(pair * width, width)
        weight_ref[:, columns] = weights.astype(jnp.bfloat16)
        dscore_ref[:, columns] = ((product - weights * delta) * scale).astype(jnp.bfloat16)
    every = range(GROUP)
    halo = pl.ds(0, 2 * CHUNK)
    grad_keys = dot(dscore_ref[halo, :], stacked(query_ref, every), PLAIN).astype(jnp.bfloat16)
    grad_values = dot(weight_ref[halo, :], stacked(grad_ref, every), PLAIN).astype(jnp.bfloat16)
    for i, total in enumerate((grad_values, grad_keys)):
        far_grad_ref[i] = total[:CHUNK]
        near_grad_ref[i] = total[CHUNK:]


def output_kernel(
    query_ref,
    grad_ref,
    far_ref,
    near_ref,
    own_ref,
    weight_ref,
    dscore_ref,
    out_ref,
    grad_query_ref,
    own_grad_ref,
):
    values_t = jnp.concatenate([far_ref[0], near_ref[0], own_ref[0]], axis=0).T
    keys_t = jnp.concatenate([far_ref[1], near_ref[1], own_ref[1]], axis=0).T
    width = 2 * CHUNK
    for pair in range(GROUP // 2):
        columns = pl.ds(pair * width, width)
        output_t = dot(values_t, weight_ref[:, columns], PLAIN).astype(jnp.bfloat16)
        grad_query_t = dot(keys_t, dscore_ref[:, columns], PLAIN).astype(jnp.bfloat16)
        for i in range(2):
            columns = pl.ds(pair * width + i * CHUNK, CHUNK)
            part = slice(i * CHUNK, (i + 1) * CHUNK)
            out_ref[:, columns] = output_t[:, part].T
            grad_query_ref[:, columns] = grad_query_t[:, part].T
    every = range(GROUP)
    own = pl.ds(2 * CHUNK, CHUNK)
    own_grad_ref[0] = dot(weight_ref[own, :], stacked(grad_ref, every), PLAIN)
    own_grad_ref[1] = dot(dscore_ref[own, :], stacked(query_ref, every), PLAIN)


def attention_specs(rows):
    wide = pl.BlockSpec((rows, GROUP * HEAD_SIZE), lambda g, *_: (0, g))
    pair = pl.BlockSpec((2, rows, HEAD_SIZE), lambda g, *_: (0, 0, g))
    window = pl.BlockSpec((WINDOW, GROUP * HEAD_SIZE), lambda g, *_: (0, g))
    return wide, pair, window


def scores_and_halo(order, place, segments, queries, grads, far, near, own):
    rows = queries.shape[0]
    wide, pair, window = attention_specs(rows)
    held = jax.ShapeDtypeStruct((WINDOW, queries.shape[1]), jnp.bfloat16)
    half = jax.ShapeDtypeStruct((2, rows, KV_WIDTH), jnp.bfloat16)
    return pl.pallas_call(
        score_kernel,
        grid_spec=pltpu.PrefetchScalarGridSpec(
            num_scalar_prefetch=2,
            grid=(KEY_VALUE_HEADS,),
            in_specs=[pl.BlockSpec(segments.shape, lambda g, *_: (0, 0)), wide, wide, pair, pair, pair],
            out_specs=[window, window, pair, pair],
            scratch_shapes=[pltpu.VMEM((WINDOW, 2 * CHUNK), jnp.float32)],
        ),
        out_shape=[held, held, half, half],
        compiler_params=pltpu.CompilerParams(vmem_limit_bytes=58 * 1024 * 1024),
        cost_estimate=pl.CostEstimate(
            flops=7 * rows * QUERY_HEADS * WINDOW * HEAD_SIZE,
            bytes_accessed=16 * rows * QUERY_HEADS * HEAD_SIZE,
            transcendentals=rows * QUERY_HEADS * WINDOW,
        ),
    )(order, place, segments, queries, grads, far, near, own)


def outputs_and_own(queries, grads, far, near, own, weights, dscores):
    rows = queries.shape[0]
    wide, pair, window = attention_specs(rows)
    like = jax.ShapeDtypeStruct(queries.shape, jnp.bfloat16)
    return pl.pallas_call(
        output_kernel,
        grid=(KEY_VALUE_HEADS,),
        in_specs=[wide, wide, pair, pair, pair, window, window],
        out_specs=[wide, wide, pair],
        out_shape=[like, like, jax.ShapeDtypeStruct((2, rows, KV_WIDTH), jnp.float32)],
        compiler_params=pltpu.CompilerParams(vmem_limit_bytes=58 * 1024 * 1024),
        cost_estimate=pl.CostEstimate(
            flops=5 * rows * QUERY_HEADS * WINDOW * HEAD_SIZE,
            bytes_accessed=20 * rows * QUERY_HEADS * HEAD_SIZE,
            transcendentals=0,
        ),
    )(queries, grads, far, near, own, weights, dscores)


def route_kernel(forward, order_ref, place_ref, held_ref, out_ref, slot_ref):
    count = order_ref.shape[0]
    for j in range(count):
        slot_ref[order_ref[j]] = j
    z, block = place_ref[0], place_ref[1]
    empty = jnp.zeros(out_ref.shape[1:], out_ref.dtype)
    for i in range(8):
        if forward:
            other = slot_ref[lax.rem(order_ref[8 * z + i] + count - 1, count)]
            index, mine, to = lax.div(other, 2), lax.rem(other, 2) == block, 2 * i
            out_ref[to + 1] = empty
        else:
            other = slot_ref[lax.rem(order_ref[2 * i + block] + 1, count)]
            index, mine, to = 2 * lax.rem(other, 8), lax.div(other, 8) == z, i

        @pl.when(mine)
        def _(to=to, index=index):
            out_ref[to] = held_ref[index]

        @pl.when(jnp.logical_not(mine))
        def _(to=to):
            out_ref[to] = empty


def route(order, place, held, forward):
    pieces = 16 if forward else 8
    whole = lambda n: pl.BlockSpec((n, *held.shape[1:]), lambda i, *_: (0, 0, 0))
    return pl.pallas_call(
        functools.partial(route_kernel, forward),
        grid_spec=pltpu.PrefetchScalarGridSpec(
            num_scalar_prefetch=2,
            grid=(1,),
            in_specs=[whole(held.shape[0])],
            out_specs=whole(pieces),
            scratch_shapes=[pltpu.SMEM((order.shape[0],), jnp.int32)],
        ),
        out_shape=jax.ShapeDtypeStruct((pieces, *held.shape[1:]), held.dtype),
        cost_estimate=pl.CostEstimate(flops=0, bytes_accessed=4 * held.size, transcendentals=0),
    )(order, place, held)


def move(value, moves):
    return lax.ppermute(value, BLOCK_AXES, moves)


def exchange(pieces, axes):
    return lax.all_to_all(pieces, axes, 0, 0)


def local(queries, keys, values, grads, segment_ids, order):
    z = lax.axis_index("z")
    block = lax.axis_index("b")
    c = lax.axis_index(BLOCK_AXES)
    place = jnp.stack([z, block, 8 * z + 2 * lax.axis_index("y") + block, c]).astype(jnp.int32)
    part = (4, CHUNK // 4, KV_WIDTH)
    whole = (CHUNK, KV_WIDTH)

    moved = move(values, [(2, 0), (3, 1)])
    own = jnp.stack([values, keys], axis=0)
    near_in = move(own, [(0, 1), (1, 2), (2, 3)])
    far_in = move(own, [(0, 2), (1, 3)])
    quarter = jnp.where(c >= 2, keys, moved).reshape(part)
    held = exchange(jnp.concatenate([quarter, quarter], axis=0), SEQ_AXES)
    held, near_in, far_in = lax.optimization_barrier((held, near_in, far_in))
    arrived = exchange(route(order, place, held, True), PLANE_AXES).reshape(4, 2, 2, *part[1:])
    arrived = (arrived[:, 0] + arrived[:, 1]).transpose(1, 0, 2, 3).reshape(2, *whole)
    before = move(arrived, [(1, 0)])
    far = jnp.where(c < 2, arrived, far_in)
    near = jnp.where(c == 0, before, near_in)

    weights, dscores, far_grad, near_grad = scores_and_halo(
        order, place, segment_ids.reshape(-1, CHUNK), queries, grads, far, near, own
    )

    before = move(near_grad, [(0, 1)])
    halo = (far_grad.astype(jnp.float32) + before.astype(jnp.float32)).astype(jnp.bfloat16)
    pieces = halo.reshape(2, *part).transpose(1, 0, 2, 3)
    pieces = jnp.broadcast_to(pieces[:, None], (4, 2, 2, *part[1:])).reshape(16, *part[1:])
    pieces, weights, dscores = lax.optimization_barrier((pieces, weights, dscores))
    held = exchange(pieces, PLANE_AXES)
    attended, grad_query, own_grad = outputs_and_own(queries, grads, far, near, own, weights, dscores)
    near_back = move(near_grad, [(1, 0), (2, 1), (3, 2)])
    far_back = move(far_grad, [(2, 0), (3, 1)])
    arrived = exchange(route(order, place, held, False), SEQ_AXES).reshape(2, *part)
    quarter = (arrived[0] + arrived[1]).reshape(whole)
    moved = move(quarter, [(0, 2), (1, 3)])

    total = own_grad + near_back.astype(jnp.float32) + far_back.astype(jnp.float32)
    key_gradient = total[1] + jnp.where(c >= 2, quarter, 0).astype(jnp.float32)
    value_gradient = total[0] + moved.astype(jnp.float32)
    return (
        attended,
        grad_query,
        key_gradient.astype(jnp.bfloat16),
        value_gradient.astype(jnp.bfloat16),
    )


def solution(mesh):
    names = ("dp", "z", "y", "b", "x", "core")
    fine = jax.sharding.Mesh(mesh.devices.reshape(-1, 2, 4, 2, 2, 2), names)
    rows = P(names, None)
    return jax.shard_map(
        local,
        mesh=fine,
        in_specs=(rows, rows, rows, rows, P("dp"), P("dp")),
        out_specs=(rows, rows, rows, rows),
        check_vma=False,
    )
```

```python
import functools
import math

import jax
import jax.numpy as jnp
from jax import lax
from jax.experimental import pallas as pl
from jax.experimental.pallas import tpu as pltpu
from jax.sharding import PartitionSpec as P

HEAD_SIZE = 128
QUERY_HEADS = 32
KEY_VALUE_HEADS = 4
GROUP = QUERY_HEADS // KEY_VALUE_HEADS
CHUNK = 128
WINDOW = 3 * CHUNK
KV_WIDTH = KEY_VALUE_HEADS * HEAD_SIZE
BLOCK_AXES = ("x", "core")
SPREAD_AXES = ("y", "x")
PLANE_AXES = ("y", "b", "x")
COUNT = 16


def usable_bias(chunk, segments_ref, bias_ref):
    query_doc = jnp.broadcast_to(segments_ref[pl.ds(chunk, 1), :], (CHUNK, CHUNK))
    for back in (2, 1, 0):
        at = chunk - back
        row = segments_ref[pl.ds(jnp.maximum(at, 0), 1), :]
        row = jnp.where(at >= 0, row, -1)
        usable = jnp.broadcast_to(row, (CHUNK, CHUNK)).T == query_doc
        if back == 0:
            usable &= lax.broadcasted_iota(jnp.int32, (CHUNK, CHUNK), 0) <= (
                lax.broadcasted_iota(jnp.int32, (CHUNK, CHUNK), 1)
            )
        tile = jnp.where(usable, 0.0, -jnp.inf).astype(jnp.float32)
        rows = pl.ds((2 - back) * CHUNK, CHUNK)
        bias_ref[rows, 0:CHUNK] = tile
        bias_ref[rows, CHUNK : 2 * CHUNK] = tile


def stacked(ref, heads):
    return jnp.concatenate(
        [ref[:, a * HEAD_SIZE : (a + 1) * HEAD_SIZE] for a in heads], axis=0
    )


LAST = (((1,), (1,)), ((), ()))
PLAIN = (((1,), (0,)), ((), ()))


def dot(left, right, dims):
    return lax.dot_general(left, right, dims, preferred_element_type=jnp.float32)


def window(info_ref, cross_ref, before_ref, far_ref, near_ref, own_ref):
    chunk = info_ref[COUNT + 3]
    far = jnp.where(chunk < 2, cross_ref[...], far_ref[...])
    near = jnp.where(chunk == 0, before_ref[...], near_ref[...])
    return tuple(jnp.concatenate([far[i], near[i], own_ref[i]], axis=0) for i in range(2))


def score_kernel(
    info_ref,
    segments_ref,
    query_ref,
    grad_ref,
    cross_ref,
    before_ref,
    far_ref,
    near_ref,
    own_ref,
    weight_ref,
    dscore_ref,
    far_grad_ref,
    near_grad_ref,
    bias_ref,
):
    @pl.when(pl.program_id(0) == 0)
    def _():
        usable_bias(info_ref[info_ref[COUNT + 2]] * 4 + info_ref[COUNT + 3], segments_ref, bias_ref)

    scale = 1.0 / math.sqrt(HEAD_SIZE)
    values, keys = window(info_ref, cross_ref, before_ref, far_ref, near_ref, own_ref)
    width = 2 * CHUNK
    pairs = GROUP // 2

    def products(pair):
        heads = (2 * pair, 2 * pair + 1)
        return (
            dot(keys, stacked(query_ref, heads), LAST),
            dot(values, stacked(grad_ref, heads), LAST),
        )

    ahead = products(0)
    for pair in range(pairs):
        scores, dprob = ahead
        if pair + 1 < pairs:
            ahead = products(pair + 1)
        scores = scores + bias_ref[...]
        top = jnp.max(scores, axis=0, keepdims=True)
        raised = jnp.exp2((scores - top) * (scale * math.log2(math.e)))
        share = 1.0 / jnp.sum(raised, axis=0, keepdims=True)
        delta = jnp.sum(raised * dprob, axis=0, keepdims=True) * share
        columns = pl.ds(pair * width, width)
        weight_ref[:, columns] = (raised * share).astype(jnp.bfloat16)
        dscore_ref[:, columns] = (raised * (share * scale) * (dprob - delta)).astype(jnp.bfloat16)
    every = range(GROUP)
    halo = pl.ds(0, 2 * CHUNK)
    grad_keys = dot(dscore_ref[halo, :], stacked(query_ref, every), PLAIN).astype(jnp.bfloat16)
    grad_values = dot(weight_ref[halo, :], stacked(grad_ref, every), PLAIN).astype(jnp.bfloat16)
    for i, total in enumerate((grad_values, grad_keys)):
        far_grad_ref[i] = total[:CHUNK]
        near_grad_ref[i] = total[CHUNK:]


def output_kernel(
    info_ref,
    query_ref,
    grad_ref,
    cross_ref,
    before_ref,
    far_ref,
    near_ref,
    own_ref,
    weight_ref,
    dscore_ref,
    out_ref,
    grad_query_ref,
    own_grad_ref,
):
    values, keys = window(info_ref, cross_ref, before_ref, far_ref, near_ref, own_ref)
    values_t, keys_t = values.T, keys.T
    width = 2 * CHUNK
    for pair in range(GROUP // 2):
        columns = pl.ds(pair * width, width)
        output_t = dot(values_t, weight_ref[:, columns], PLAIN).astype(jnp.bfloat16)
        grad_query_t = dot(keys_t, dscore_ref[:, columns], PLAIN).astype(jnp.bfloat16)
        for i in range(2):
            columns = pl.ds(pair * width + i * CHUNK, CHUNK)
            part = slice(i * CHUNK, (i + 1) * CHUNK)
            out_ref[:, columns] = output_t[:, part].T
            grad_query_ref[:, columns] = grad_query_t[:, part].T
    every = range(GROUP)
    own = pl.ds(2 * CHUNK, CHUNK)
    own_grad_ref[0] = dot(weight_ref[own, :], stacked(grad_ref, every), PLAIN)
    own_grad_ref[1] = dot(dscore_ref[own, :], stacked(query_ref, every), PLAIN)


def attention_specs(rows):
    wide = pl.BlockSpec((rows, GROUP * HEAD_SIZE), lambda g, *_: (0, g))
    pair = pl.BlockSpec((2, rows, HEAD_SIZE), lambda g, *_: (0, 0, g))
    tall = pl.BlockSpec((WINDOW, GROUP * HEAD_SIZE), lambda g, *_: (0, g))
    return wide, pair, tall


def scores_and_halo(info, segments, queries, grads, pairs):
    rows = queries.shape[0]
    wide, pair, tall = attention_specs(rows)
    held = jax.ShapeDtypeStruct((WINDOW, queries.shape[1]), jnp.bfloat16)
    half = jax.ShapeDtypeStruct((2, rows, KV_WIDTH), jnp.bfloat16)
    return pl.pallas_call(
        score_kernel,
        grid_spec=pltpu.PrefetchScalarGridSpec(
            num_scalar_prefetch=1,
            grid=(KEY_VALUE_HEADS,),
            in_specs=[pl.BlockSpec(segments.shape, lambda g, *_: (0, 0)), wide, wide] + [pair] * 5,
            out_specs=[tall, tall, pair, pair],
            scratch_shapes=[pltpu.VMEM((WINDOW, 2 * CHUNK), jnp.float32)],
        ),
        out_shape=[held, held, half, half],
        compiler_params=pltpu.CompilerParams(vmem_limit_bytes=58 * 1024 * 1024),
        cost_estimate=pl.CostEstimate(
            flops=7 * rows * QUERY_HEADS * WINDOW * HEAD_SIZE,
            bytes_accessed=16 * rows * QUERY_HEADS * HEAD_SIZE,
            transcendentals=rows * QUERY_HEADS * WINDOW,
        ),
    )(info, segments, queries, grads, *pairs)


def outputs_and_own(info, queries, grads, pairs, weights, dscores):
    rows = queries.shape[0]
    wide, pair, tall = attention_specs(rows)
    like = jax.ShapeDtypeStruct(queries.shape, jnp.bfloat16)
    return pl.pallas_call(
        output_kernel,
        grid_spec=pltpu.PrefetchScalarGridSpec(
            num_scalar_prefetch=1,
            grid=(KEY_VALUE_HEADS,),
            in_specs=[wide, wide] + [pair] * 5 + [tall, tall],
            out_specs=[wide, wide, pair],
        ),
        out_shape=[like, like, jax.ShapeDtypeStruct((2, rows, KV_WIDTH), jnp.float32)],
        compiler_params=pltpu.CompilerParams(vmem_limit_bytes=58 * 1024 * 1024),
        cost_estimate=pl.CostEstimate(
            flops=5 * rows * QUERY_HEADS * WINDOW * HEAD_SIZE,
            bytes_accessed=20 * rows * QUERY_HEADS * HEAD_SIZE,
            transcendentals=0,
        ),
    )(info, queries, grads, *pairs, weights, dscores)


def slots_in_order(info_ref, slot_ref):
    for j in range(COUNT):
        slot_ref[info_ref[j]] = j


def route_forward_kernel(info_ref, here_ref, there_ref, out_ref, slot_ref):
    slots_in_order(info_ref, slot_ref)
    z, block = info_ref[COUNT], info_ref[COUNT + 1]
    empty = jnp.zeros(out_ref.shape[1:], out_ref.dtype)
    for i in range(8):
        source = slot_ref[lax.rem(info_ref[8 * z + i] + COUNT - 1, COUNT)]
        mine = lax.rem(source, 2) == block
        near = lax.div(source, 8) == z
        y = lax.rem(lax.div(source, 2), 4)
        out_ref[2 * i + 1] = empty

        @pl.when(jnp.logical_and(mine, near))
        def _(i=i, y=y):
            out_ref[2 * i] = here_ref[y]

        @pl.when(jnp.logical_and(mine, jnp.logical_not(near)))
        def _(i=i, y=y):
            out_ref[2 * i] = there_ref[y]

        @pl.when(jnp.logical_not(mine))
        def _(i=i):
            out_ref[2 * i] = empty


def route_back_kernel(info_ref, held_ref, here_ref, there_ref, slot_ref):
    slots_in_order(info_ref, slot_ref)
    z, block = info_ref[COUNT], info_ref[COUNT + 1]
    empty = jnp.zeros(here_ref.shape[1:], here_ref.dtype)
    for half, out_ref in ((z, here_ref), (1 - z, there_ref)):
        for y in range(4):
            after = slot_ref[lax.rem(info_ref[8 * half + 2 * y + block] + 1, COUNT)]
            mine = lax.div(after, 8) == z

            @pl.when(mine)
            def _(out_ref=out_ref, y=y, after=after):
                out_ref[y] = held_ref[2 * lax.rem(after, 8)]

            @pl.when(jnp.logical_not(mine))
            def _(out_ref=out_ref, y=y):
                out_ref[y] = empty


def route(kernel, info, operands, counts):
    shape = operands[0].shape[1:]
    whole = lambda n: pl.BlockSpec((n, *shape), lambda i, *_: (0, 0, 0))
    return pl.pallas_call(
        kernel,
        grid_spec=pltpu.PrefetchScalarGridSpec(
            num_scalar_prefetch=1,
            grid=(1,),
            in_specs=[whole(t.shape[0]) for t in operands],
            out_specs=[whole(n) for n in counts],
            scratch_shapes=[pltpu.SMEM((COUNT,), jnp.int32)],
        ),
        out_shape=[jax.ShapeDtypeStruct((n, *shape), jnp.bfloat16) for n in counts],
        cost_estimate=pl.CostEstimate(flops=0, bytes_accessed=1 << 20, transcendentals=0),
    )(info, *operands)


def move(value, moves):
    return lax.ppermute(value, BLOCK_AXES, moves)


def exchange(pieces, axes):
    return lax.all_to_all(pieces, axes, 0, 0)


def across(value):
    return lax.ppermute(value, "z", [(0, 1), (1, 0)])


def local(queries, keys, values, grads, segment_ids, order):
    z = lax.axis_index("z")
    block = lax.axis_index("b")
    c = lax.axis_index(BLOCK_AXES)
    place = [z, block, 8 * z + 2 * lax.axis_index("y") + block, c]
    info = jnp.concatenate([order, jnp.stack(place).astype(jnp.int32)])
    part = (4, CHUNK // 4, KV_WIDTH)
    whole = (CHUNK, KV_WIDTH)
    own = jnp.stack([values, keys], axis=0)

    pieces = own.reshape(2, *part).transpose(1, 0, 2, 3).reshape(8, *part[1:])
    here = exchange(pieces, SPREAD_AXES).reshape(4, 2, *part[1:])[:, 1]
    there = across(here)
    near_in = move(own, [(0, 1), (1, 2), (2, 3)])
    far_in = move(own, [(0, 2), (1, 3)])
    there, near_in, far_in = lax.optimization_barrier((there, near_in, far_in))
    (pieces,) = route(route_forward_kernel, info, (here, there), (16,))
    arrived = exchange(pieces, PLANE_AXES).reshape(4, 2, 2, *part[1:])
    cross = (arrived[:, 0] + arrived[:, 1]).transpose(1, 0, 2, 3).reshape(2, *whole)
    pairs = (cross, move(cross, [(1, 0)]), far_in, near_in, own)

    weights, dscores, far_grad, near_grad = scores_and_halo(
        info, segment_ids.reshape(-1, CHUNK), queries, grads, pairs
    )

    before = move(near_grad, [(0, 1)])
    halo = (far_grad.astype(jnp.float32) + before.astype(jnp.float32)).astype(jnp.bfloat16)
    pieces = halo.reshape(2, *part).transpose(1, 0, 2, 3)
    pieces = jnp.broadcast_to(pieces[:, None], (4, 2, 2, *part[1:])).reshape(16, *part[1:])
    held = exchange(pieces, PLANE_AXES)
    here, there = route(route_back_kernel, info, (held,), (4, 4))
    there, weights, dscores = lax.optimization_barrier((there, weights, dscores))
    there = across(there)
    attended, grad_query, own_grad = outputs_and_own(info, queries, grads, pairs, weights, dscores)
    near_back = move(near_grad, [(1, 0), (2, 1), (3, 2)])
    far_back = move(far_grad, [(2, 0), (3, 1)])
    pieces = jnp.broadcast_to((here + there)[:, None], (4, 2, *part[1:])).reshape(8, *part[1:])
    late = exchange(pieces, SPREAD_AXES).reshape(4, 2, *part[1:]).transpose(1, 0, 2, 3)
    late = jnp.where(c >= 2, late.reshape(2, *whole), 0)

    total = own_grad + near_back.astype(jnp.float32) + far_back.astype(jnp.float32)
    value_gradient = total[0] + late[0].astype(jnp.float32)
    key_gradient = total[1] + late[1].astype(jnp.float32)
    return (
        attended,
        grad_query,
        key_gradient.astype(jnp.bfloat16),
        value_gradient.astype(jnp.bfloat16),
    )


def solution(mesh):
    names = ("dp", "z", "y", "b", "x", "core")
    fine = jax.sharding.Mesh(mesh.devices.reshape(-1, 2, 4, 2, 2, 2), names)
    rows = P(names, None)
    return jax.shard_map(
        local,
        mesh=fine,
        in_specs=(rows, rows, rows, rows, P("dp"), P("dp")),
        out_specs=(rows, rows, rows, rows),
        check_vma=False,
    )
```

```python
import functools
import math

import jax
import jax.numpy as jnp
from jax import lax
from jax.experimental import pallas as pl
from jax.experimental.pallas import tpu as pltpu
from jax.sharding import PartitionSpec as P

HEAD_SIZE = 128
QUERY_HEADS = 32
KEY_VALUE_HEADS = 4
GROUP = QUERY_HEADS // KEY_VALUE_HEADS
CHUNK = 128
WINDOW = 3 * CHUNK
KV_WIDTH = KEY_VALUE_HEADS * HEAD_SIZE
BLOCK_AXES = ("x", "core")
SPREAD_AXES = ("x", "y")
PLANE_AXES = ("x", "y", "b")
COUNT = 16


def usable_bias(chunk, segments_ref, bias_ref):
    query_doc = jnp.broadcast_to(segments_ref[pl.ds(chunk, 1), :], (CHUNK, CHUNK))
    for back in (2, 1, 0):
        at = chunk - back
        row = segments_ref[pl.ds(jnp.maximum(at, 0), 1), :]
        row = jnp.where(at >= 0, row, -1)
        usable = jnp.broadcast_to(row, (CHUNK, CHUNK)).T == query_doc
        if back == 0:
            usable &= lax.broadcasted_iota(jnp.int32, (CHUNK, CHUNK), 0) <= (
                lax.broadcasted_iota(jnp.int32, (CHUNK, CHUNK), 1)
            )
        tile = jnp.where(usable, 0.0, -jnp.inf).astype(jnp.float32)
        rows = pl.ds((2 - back) * CHUNK, CHUNK)
        bias_ref[rows, 0:CHUNK] = tile
        bias_ref[rows, CHUNK : 2 * CHUNK] = tile


def stacked(ref, heads):
    return jnp.concatenate(
        [ref[:, a * HEAD_SIZE : (a + 1) * HEAD_SIZE] for a in heads], axis=0
    )


LAST = (((1,), (1,)), ((), ()))
PLAIN = (((1,), (0,)), ((), ()))


def dot(left, right, dims):
    return lax.dot_general(left, right, dims, preferred_element_type=jnp.float32)


def window(info_ref, cross_ref, before_ref, far_ref, near_ref, own_ref):
    chunk = info_ref[COUNT + 3]
    far = jnp.where(chunk < 2, cross_ref[...], far_ref[...])
    near = jnp.where(chunk == 0, before_ref[...], near_ref[...])
    return tuple(jnp.concatenate([far[i], near[i], own_ref[i]], axis=0) for i in range(2))


def score_kernel(
    info_ref,
    segments_ref,
    query_ref,
    grad_ref,
    cross_ref,
    before_ref,
    far_ref,
    near_ref,
    own_ref,
    weight_ref,
    dscore_ref,
    far_grad_ref,
    near_grad_ref,
    bias_ref,
):
    @pl.when(pl.program_id(0) == 0)
    def _():
        usable_bias(info_ref[info_ref[COUNT + 2]] * 4 + info_ref[COUNT + 3], segments_ref, bias_ref)

    scale = 1.0 / math.sqrt(HEAD_SIZE)
    values, keys = window(info_ref, cross_ref, before_ref, far_ref, near_ref, own_ref)
    width = 2 * CHUNK
    pairs = GROUP // 2

    def products(pair):
        heads = (2 * pair, 2 * pair + 1)
        return (
            dot(keys, stacked(query_ref, heads), LAST),
            dot(values, stacked(grad_ref, heads), LAST),
        )

    ahead = products(0)
    for pair in range(pairs):
        scores, dprob = ahead
        if pair + 1 < pairs:
            ahead = products(pair + 1)
        scores = scores + bias_ref[...]
        top = jnp.max(scores, axis=0, keepdims=True)
        raised = jnp.exp2((scores - top) * (scale * math.log2(math.e)))
        share = 1.0 / jnp.sum(raised, axis=0, keepdims=True)
        delta = jnp.sum(raised * dprob, axis=0, keepdims=True) * share
        columns = pl.ds(pair * width, width)
        weight_ref[:, columns] = (raised * share).astype(jnp.bfloat16)
        dscore_ref[:, columns] = (raised * (share * scale) * (dprob - delta)).astype(jnp.bfloat16)
    every = range(GROUP)
    halo = pl.ds(0, 2 * CHUNK)
    grad_keys = dot(dscore_ref[halo, :], stacked(query_ref, every), PLAIN).astype(jnp.bfloat16)
    grad_values = dot(weight_ref[halo, :], stacked(grad_ref, every), PLAIN).astype(jnp.bfloat16)
    for i, total in enumerate((grad_values, grad_keys)):
        far_grad_ref[i] = total[:CHUNK]
        near_grad_ref[i] = total[CHUNK:]


def output_kernel(
    info_ref,
    query_ref,
    grad_ref,
    cross_ref,
    before_ref,
    far_ref,
    near_ref,
    own_ref,
    weight_ref,
    dscore_ref,
    out_ref,
    grad_query_ref,
    own_grad_ref,
):
    values, keys = window(info_ref, cross_ref, before_ref, far_ref, near_ref, own_ref)
    values_t, keys_t = values.T, keys.T
    width = 2 * CHUNK
    for pair in range(GROUP // 2):
        columns = pl.ds(pair * width, width)
        output_t = dot(values_t, weight_ref[:, columns], PLAIN).astype(jnp.bfloat16)
        grad_query_t = dot(keys_t, dscore_ref[:, columns], PLAIN).astype(jnp.bfloat16)
        for i in range(2):
            columns = pl.ds(pair * width + i * CHUNK, CHUNK)
            part = slice(i * CHUNK, (i + 1) * CHUNK)
            out_ref[:, columns] = output_t[:, part].T
            grad_query_ref[:, columns] = grad_query_t[:, part].T
    every = range(GROUP)
    own = pl.ds(2 * CHUNK, CHUNK)
    own_grad_ref[0] = dot(weight_ref[own, :], stacked(grad_ref, every), PLAIN)
    own_grad_ref[1] = dot(dscore_ref[own, :], stacked(query_ref, every), PLAIN)


def attention_specs(rows):
    wide = pl.BlockSpec((rows, GROUP * HEAD_SIZE), lambda g, *_: (0, g))
    pair = pl.BlockSpec((2, rows, HEAD_SIZE), lambda g, *_: (0, 0, g))
    tall = pl.BlockSpec((WINDOW, GROUP * HEAD_SIZE), lambda g, *_: (0, g))
    return wide, pair, tall


def scores_and_halo(info, segments, queries, grads, pairs):
    rows = queries.shape[0]
    wide, pair, tall = attention_specs(rows)
    held = jax.ShapeDtypeStruct((WINDOW, queries.shape[1]), jnp.bfloat16)
    half = jax.ShapeDtypeStruct((2, rows, KV_WIDTH), jnp.bfloat16)
    return pl.pallas_call(
        score_kernel,
        grid_spec=pltpu.PrefetchScalarGridSpec(
            num_scalar_prefetch=1,
            grid=(KEY_VALUE_HEADS,),
            in_specs=[pl.BlockSpec(segments.shape, lambda g, *_: (0, 0)), wide, wide] + [pair] * 5,
            out_specs=[tall, tall, pair, pair],
            scratch_shapes=[pltpu.VMEM((WINDOW, 2 * CHUNK), jnp.float32)],
        ),
        out_shape=[held, held, half, half],
        compiler_params=pltpu.CompilerParams(vmem_limit_bytes=58 * 1024 * 1024),
        cost_estimate=pl.CostEstimate(
            flops=7 * rows * QUERY_HEADS * WINDOW * HEAD_SIZE,
            bytes_accessed=16 * rows * QUERY_HEADS * HEAD_SIZE,
            transcendentals=rows * QUERY_HEADS * WINDOW,
        ),
    )(info, segments, queries, grads, *pairs)


def outputs_and_own(info, queries, grads, pairs, weights, dscores):
    rows = queries.shape[0]
    wide, pair, tall = attention_specs(rows)
    like = jax.ShapeDtypeStruct(queries.shape, jnp.bfloat16)
    return pl.pallas_call(
        output_kernel,
        grid_spec=pltpu.PrefetchScalarGridSpec(
            num_scalar_prefetch=1,
            grid=(KEY_VALUE_HEADS,),
            in_specs=[wide, wide] + [pair] * 5 + [tall, tall],
            out_specs=[wide, wide, pair],
        ),
        out_shape=[like, like, jax.ShapeDtypeStruct((2, rows, KV_WIDTH), jnp.float32)],
        compiler_params=pltpu.CompilerParams(vmem_limit_bytes=58 * 1024 * 1024),
        cost_estimate=pl.CostEstimate(
            flops=5 * rows * QUERY_HEADS * WINDOW * HEAD_SIZE,
            bytes_accessed=20 * rows * QUERY_HEADS * HEAD_SIZE,
            transcendentals=0,
        ),
    )(info, queries, grads, *pairs, weights, dscores)


def slots_in_order(info_ref, slot_ref):
    for j in range(COUNT):
        slot_ref[info_ref[j]] = j


def route_forward_kernel(info_ref, here_ref, there_ref, out_ref, slot_ref):
    slots_in_order(info_ref, slot_ref)
    z, block = info_ref[COUNT], info_ref[COUNT + 1]
    empty = jnp.zeros(out_ref.shape[1:], out_ref.dtype)
    for i in range(8):
        source = slot_ref[lax.rem(info_ref[8 * z + i] + COUNT - 1, COUNT)]
        mine = lax.rem(source, 2) == block
        near = lax.div(source, 8) == z
        y = lax.rem(lax.div(source, 2), 4)
        out_ref[8 + i] = empty

        @pl.when(jnp.logical_and(mine, near))
        def _(i=i, y=y):
            out_ref[i] = here_ref[y]

        @pl.when(jnp.logical_and(mine, jnp.logical_not(near)))
        def _(i=i, y=y):
            out_ref[i] = there_ref[y]

        @pl.when(jnp.logical_not(mine))
        def _(i=i):
            out_ref[i] = empty


def route_back_kernel(info_ref, held_ref, here_ref, there_ref, slot_ref):
    slots_in_order(info_ref, slot_ref)
    z, block = info_ref[COUNT], info_ref[COUNT + 1]
    empty = jnp.zeros(here_ref.shape[1:], here_ref.dtype)
    for half, out_ref in ((z, here_ref), (1 - z, there_ref)):
        for y in range(4):
            after = slot_ref[lax.rem(info_ref[8 * half + 2 * y + block] + 1, COUNT)]
            mine = lax.div(after, 8) == z

            @pl.when(mine)
            def _(out_ref=out_ref, y=y, after=after):
                out_ref[y] = held_ref[lax.rem(after, 8)]

            @pl.when(jnp.logical_not(mine))
            def _(out_ref=out_ref, y=y):
                out_ref[y] = empty


def route(kernel, info, operands, counts):
    shape = operands[0].shape[1:]
    in_vmem = pl.BlockSpec(memory_space=pltpu.VMEM)
    return pl.pallas_call(
        kernel,
        in_specs=[pl.BlockSpec(memory_space=pltpu.SMEM)] + [in_vmem] * len(operands),
        out_specs=[in_vmem] * len(counts),
        out_shape=[jax.ShapeDtypeStruct((n, *shape), jnp.bfloat16) for n in counts],
        scratch_shapes=[pltpu.SMEM((COUNT,), jnp.int32)],
        compiler_params=pltpu.CompilerParams(vmem_limit_bytes=4 * 1024 * 1024),
        cost_estimate=pl.CostEstimate(flops=0, bytes_accessed=1 << 20, transcendentals=0),
    )(info, *operands)


def move(value, moves):
    return lax.ppermute(value, BLOCK_AXES, moves)


def exchange(pieces, axes):
    return lax.all_to_all(pieces, axes, 0, 0)


def across(value):
    return lax.ppermute(value, "z", [(0, 1), (1, 0)])


def local(queries, keys, values, grads, segment_ids, order):
    z = lax.axis_index("z")
    block = lax.axis_index("b")
    c = lax.axis_index(BLOCK_AXES)
    place = [z, block, 8 * z + 2 * lax.axis_index("y") + block, c]
    info = jnp.concatenate([order, jnp.stack(place).astype(jnp.int32)])
    part = (4, CHUNK // 4, KV_WIDTH)
    whole = (CHUNK, KV_WIDTH)
    own = jnp.stack([values, keys], axis=0)

    here = exchange(own.reshape(8, *part[1:]), SPREAD_AXES).reshape(2, *part)[1]
    there = across(here)
    near_in = move(own, [(0, 1), (1, 2), (2, 3)])
    far_in = move(own, [(0, 2), (1, 3)])
    there, near_in, far_in = lax.optimization_barrier((there, near_in, far_in))
    (pieces,) = route(route_forward_kernel, info, (here, there), (16,))
    arrived = exchange(pieces, PLANE_AXES).reshape(2, 4, 2, *part[1:])
    cross = (arrived[:, :, 0] + arrived[:, :, 1]).reshape(2, *whole)
    pairs = (cross, move(cross, [(1, 0)]), far_in, near_in, own)

    weights, dscores, far_grad, near_grad = scores_and_halo(
        info, segment_ids.reshape(-1, CHUNK), queries, grads, pairs
    )

    before = move(near_grad, [(0, 1)])
    halo = (far_grad.astype(jnp.float32) + before.astype(jnp.float32)).astype(jnp.bfloat16)
    pieces = jnp.broadcast_to(halo.reshape(2, 4, 1, *part[1:]), (2, 4, 2, *part[1:]))
    pieces, weights, dscores = lax.optimization_barrier((pieces, weights, dscores))
    held = exchange(pieces.reshape(16, *part[1:]), PLANE_AXES)
    attended, grad_query, own_grad = outputs_and_own(info, queries, grads, pairs, weights, dscores)
    held, own_grad = lax.optimization_barrier((held, own_grad))
    here, there = route(route_back_kernel, info, (held,), (4, 4))
    there = across(there)
    near_back = move(near_grad, [(1, 0), (2, 1), (3, 2)])
    far_back = move(far_grad, [(2, 0), (3, 1)])
    pieces = jnp.broadcast_to(here + there, (2, *part)).reshape(8, *part[1:])
    late = exchange(pieces, SPREAD_AXES).reshape(2, *whole)
    late = jnp.where(c >= 2, late, 0)

    total = own_grad + near_back.astype(jnp.float32) + far_back.astype(jnp.float32)
    value_gradient = total[0] + late[0].astype(jnp.float32)
    key_gradient = total[1] + late[1].astype(jnp.float32)
    return (
        attended,
        grad_query,
        key_gradient.astype(jnp.bfloat16),
        value_gradient.astype(jnp.bfloat16),
    )


def solution(mesh):
    names = ("dp", "z", "y", "b", "x", "core")
    fine = jax.sharding.Mesh(mesh.devices.reshape(-1, 2, 4, 2, 2, 2), names)
    rows = P(names, None)
    return jax.shard_map(
        local,
        mesh=fine,
        in_specs=(rows, rows, rows, rows, P("dp"), P("dp")),
        out_specs=(rows, rows, rows, rows),
        check_vma=False,
    )
```

```python
import functools
import math

import jax
import jax.numpy as jnp
from jax import lax
from jax.experimental import pallas as pl
from jax.experimental.pallas import tpu as pltpu
from jax.sharding import PartitionSpec as P

HEAD_SIZE = 128
QUERY_HEADS = 32
KEY_VALUE_HEADS = 4
GROUP = QUERY_HEADS // KEY_VALUE_HEADS
CHUNK = 128
WINDOW = 3 * CHUNK
KV_WIDTH = KEY_VALUE_HEADS * HEAD_SIZE
BLOCK_AXES = ("x", "core")
SPREAD_AXES = ("x", "y")
PLANE_AXES = ("x", "y", "b")
SCALE = 1.0 / math.sqrt(HEAD_SIZE)
COUNT = 16


def usable_bias(chunk, segments_ref, bias_ref):
    query_doc = jnp.broadcast_to(segments_ref[pl.ds(chunk, 1), :], (CHUNK, CHUNK))
    for back in (2, 1, 0):
        at = chunk - back
        row = segments_ref[pl.ds(jnp.maximum(at, 0), 1), :]
        row = jnp.where(at >= 0, row, -1)
        usable = jnp.broadcast_to(row, (CHUNK, CHUNK)).T == query_doc
        if back == 0:
            usable &= lax.broadcasted_iota(jnp.int32, (CHUNK, CHUNK), 0) <= (
                lax.broadcasted_iota(jnp.int32, (CHUNK, CHUNK), 1)
            )
        tile = jnp.where(usable, 0.0, -jnp.inf).astype(jnp.float32)
        rows = pl.ds((2 - back) * CHUNK, CHUNK)
        bias_ref[rows, 0:CHUNK] = tile
        bias_ref[rows, CHUNK : 2 * CHUNK] = tile


def stacked(ref, heads):
    return jnp.concatenate(
        [ref[:, a * HEAD_SIZE : (a + 1) * HEAD_SIZE] for a in heads], axis=0
    )


LAST = (((1,), (1,)), ((), ()))
PLAIN = (((1,), (0,)), ((), ()))


def dot(left, right, dims):
    return lax.dot_general(left, right, dims, preferred_element_type=jnp.float32)


def window(info_ref, cross_ref, before_ref, far_ref, near_ref, own_ref):
    chunk = info_ref[COUNT + 3]
    far = jnp.where(chunk < 2, cross_ref[...], far_ref[...])
    near = jnp.where(chunk == 0, before_ref[...], near_ref[...])
    return tuple(jnp.concatenate([far[i], near[i], own_ref[i]], axis=0) for i in range(2))


def score_kernel(
    info_ref,
    segments_ref,
    query_ref,
    grad_ref,
    cross_ref,
    before_ref,
    far_ref,
    near_ref,
    own_ref,
    weight_ref,
    dscore_ref,
    far_grad_ref,
    near_grad_ref,
    bias_ref,
):
    @pl.when(pl.program_id(0) == 0)
    def _():
        usable_bias(info_ref[info_ref[COUNT + 2]] * 4 + info_ref[COUNT + 3], segments_ref, bias_ref)

    values, keys = window(info_ref, cross_ref, before_ref, far_ref, near_ref, own_ref)
    width = 2 * CHUNK
    pairs = GROUP // 2

    def products(pair):
        heads = (2 * pair, 2 * pair + 1)
        return (
            dot(keys, stacked(query_ref, heads), LAST),
            dot(values, stacked(grad_ref, heads), LAST),
        )

    ahead = products(0)
    for pair in range(pairs):
        scores, dprob = ahead
        if pair + 1 < pairs:
            ahead = products(pair + 1)
        scores = scores + bias_ref[...]
        top = jnp.max(scores, axis=0, keepdims=True)
        raised = jnp.exp2((scores - top) * (SCALE * math.log2(math.e)))
        share = 1.0 / jnp.sum(raised, axis=0, keepdims=True)
        delta = jnp.sum(raised * dprob, axis=0, keepdims=True) * share
        weights = raised * share
        columns = pl.ds(pair * width, width)
        weight_ref[:, columns] = weights.astype(jnp.bfloat16)
        dscore_ref[:, columns] = (weights * (dprob - delta)).astype(jnp.bfloat16)
    every = range(GROUP)
    halo = pl.ds(0, 2 * CHUNK)
    grad_keys = (dot(dscore_ref[halo, :], stacked(query_ref, every), PLAIN) * SCALE).astype(jnp.bfloat16)
    grad_values = dot(weight_ref[halo, :], stacked(grad_ref, every), PLAIN).astype(jnp.bfloat16)
    for i, total in enumerate((grad_values, grad_keys)):
        far_grad_ref[i] = total[:CHUNK]
        near_grad_ref[i] = total[CHUNK:]


def product_kernel(which, info_ref, row_ref, *refs):
    *pair_refs, factor_ref, out_ref, own_grad_ref = refs
    window_t = window(info_ref, *pair_refs)[which].T
    factor = (1.0, SCALE)[which]
    width = 2 * CHUNK
    for pair in range(GROUP // 2):
        columns = pl.ds(pair * width, width)
        rows_t = (dot(window_t, factor_ref[:, columns], PLAIN) * factor).astype(jnp.bfloat16)
        for i in range(2):
            columns = pl.ds(pair * width + i * CHUNK, CHUNK)
            out_ref[:, columns] = rows_t[:, i * CHUNK : (i + 1) * CHUNK].T
    own = factor_ref[pl.ds(2 * CHUNK, CHUNK), :]
    own_grad_ref[...] = dot(own, stacked(row_ref, range(GROUP)), PLAIN) * factor


def attention_specs(rows):
    wide = pl.BlockSpec((rows, GROUP * HEAD_SIZE), lambda g, *_: (0, g))
    pair = pl.BlockSpec((2, rows, HEAD_SIZE), lambda g, *_: (0, 0, g))
    tall = pl.BlockSpec((WINDOW, GROUP * HEAD_SIZE), lambda g, *_: (0, g))
    return wide, pair, tall


def scores_and_halo(info, segments, queries, grads, pairs):
    rows = queries.shape[0]
    wide, pair, tall = attention_specs(rows)
    held = jax.ShapeDtypeStruct((WINDOW, queries.shape[1]), jnp.bfloat16)
    half = jax.ShapeDtypeStruct((2, rows, KV_WIDTH), jnp.bfloat16)
    return pl.pallas_call(
        score_kernel,
        grid_spec=pltpu.PrefetchScalarGridSpec(
            num_scalar_prefetch=1,
            grid=(KEY_VALUE_HEADS,),
            in_specs=[pl.BlockSpec(segments.shape, lambda g, *_: (0, 0)), wide, wide] + [pair] * 5,
            out_specs=[tall, tall, pair, pair],
            scratch_shapes=[pltpu.VMEM((WINDOW, 2 * CHUNK), jnp.float32)],
        ),
        out_shape=[held, held, half, half],
        compiler_params=pltpu.CompilerParams(vmem_limit_bytes=58 * 1024 * 1024),
        cost_estimate=pl.CostEstimate(
            flops=7 * rows * QUERY_HEADS * WINDOW * HEAD_SIZE,
            bytes_accessed=16 * rows * QUERY_HEADS * HEAD_SIZE,
            transcendentals=rows * QUERY_HEADS * WINDOW,
        ),
    )(info, segments, queries, grads, *pairs)


def output_and_own(which, info, rows_in, pairs, factors):
    rows = rows_in.shape[0]
    wide, pair, tall = attention_specs(rows)
    narrow = pl.BlockSpec((rows, HEAD_SIZE), lambda g, *_: (0, g))
    return pl.pallas_call(
        functools.partial(product_kernel, which),
        grid_spec=pltpu.PrefetchScalarGridSpec(
            num_scalar_prefetch=1,
            grid=(KEY_VALUE_HEADS,),
            in_specs=[wide] + [pair] * 5 + [tall],
            out_specs=[wide, narrow],
        ),
        out_shape=[
            jax.ShapeDtypeStruct(rows_in.shape, jnp.bfloat16),
            jax.ShapeDtypeStruct((rows, KV_WIDTH), jnp.float32),
        ],
        compiler_params=pltpu.CompilerParams(vmem_limit_bytes=58 * 1024 * 1024),
        cost_estimate=pl.CostEstimate(
            flops=5 * rows * QUERY_HEADS * WINDOW * HEAD_SIZE // 2,
            bytes_accessed=10 * rows * QUERY_HEADS * HEAD_SIZE,
            transcendentals=0,
        ),
    )(info, rows_in, *pairs, factors)


def pair_kernel(values_ref, keys_ref, out_ref, sems):
    copies = [
        pltpu.make_async_copy(ref, out_ref.at[i], sems.at[i])
        for i, ref in enumerate((values_ref, keys_ref))
    ]
    for copy in copies:
        copy.start()
    for copy in copies:
        copy.wait()


def paired(values, keys):
    return pl.pallas_call(
        pair_kernel,
        in_specs=[pl.BlockSpec(memory_space=pl.ANY)] * 2,
        out_specs=pl.BlockSpec(memory_space=pltpu.VMEM),
        out_shape=jax.ShapeDtypeStruct((2, *values.shape), values.dtype),
        scratch_shapes=[pltpu.SemaphoreType.DMA((2,))],
        compiler_params=pltpu.CompilerParams(vmem_limit_bytes=4 * 1024 * 1024),
    )(values, keys)


def join_kernel(far_ref, before_ref, out_ref):
    rows = CHUNK // 4
    for i in range(2):
        for y in range(4):
            part = pl.ds(y * rows, rows)
            total = far_ref[i, part, :].astype(jnp.float32) + before_ref[i, part, :].astype(jnp.float32)
            for b in range(2):
                out_ref[8 * i + 2 * y + b] = total.astype(jnp.bfloat16)


def joined(far_grad, before):
    in_vmem = pl.BlockSpec(memory_space=pltpu.VMEM)
    return pl.pallas_call(
        join_kernel,
        in_specs=[in_vmem] * 2,
        out_specs=in_vmem,
        out_shape=jax.ShapeDtypeStruct((16, CHUNK // 4, KV_WIDTH), jnp.bfloat16),
        compiler_params=pltpu.CompilerParams(vmem_limit_bytes=4 * 1024 * 1024),
    )(far_grad, before)


def slots_in_order(info_ref, slot_ref):
    for j in range(COUNT):
        slot_ref[info_ref[j]] = j


def route_forward_kernel(info_ref, here_ref, there_ref, out_ref, slot_ref):
    slots_in_order(info_ref, slot_ref)
    z, block = info_ref[COUNT], info_ref[COUNT + 1]
    empty = jnp.zeros(out_ref.shape[1:], out_ref.dtype)
    for i in range(8):
        source = slot_ref[lax.rem(info_ref[8 * z + i] + COUNT - 1, COUNT)]
        mine = lax.rem(source, 2) == block
        near = lax.div(source, 8) == z
        y = lax.rem(lax.div(source, 2), 4)
        out_ref[8 + i] = empty

        @pl.when(jnp.logical_and(mine, near))
        def _(i=i, y=y):
            out_ref[i] = here_ref[y]

        @pl.when(jnp.logical_and(mine, jnp.logical_not(near)))
        def _(i=i, y=y):
            out_ref[i] = there_ref[y]

        @pl.when(jnp.logical_not(mine))
        def _(i=i):
            out_ref[i] = empty


def route_back_kernel(info_ref, held_ref, here_ref, there_ref, slot_ref):
    slots_in_order(info_ref, slot_ref)
    z, block = info_ref[COUNT], info_ref[COUNT + 1]
    empty = jnp.zeros(here_ref.shape[1:], here_ref.dtype)
    for half, out_ref in ((z, here_ref), (1 - z, there_ref)):
        for y in range(4):
            after = slot_ref[lax.rem(info_ref[8 * half + 2 * y + block] + 1, COUNT)]
            mine = lax.div(after, 8) == z

            @pl.when(mine)
            def _(out_ref=out_ref, y=y, after=after):
                out_ref[y] = held_ref[lax.rem(after, 8)]

            @pl.when(jnp.logical_not(mine))
            def _(out_ref=out_ref, y=y):
                out_ref[y] = empty


def route(kernel, info, operands, counts):
    shape = operands[0].shape[1:]
    in_vmem = pl.BlockSpec(memory_space=pltpu.VMEM)
    return pl.pallas_call(
        kernel,
        in_specs=[pl.BlockSpec(memory_space=pltpu.SMEM)] + [in_vmem] * len(operands),
        out_specs=[in_vmem] * len(counts),
        out_shape=[jax.ShapeDtypeStruct((n, *shape), jnp.bfloat16) for n in counts],
        scratch_shapes=[pltpu.SMEM((COUNT,), jnp.int32)],
        compiler_params=pltpu.CompilerParams(vmem_limit_bytes=4 * 1024 * 1024),
        cost_estimate=pl.CostEstimate(flops=0, bytes_accessed=1 << 20, transcendentals=0),
    )(info, *operands)


def move(value, moves):
    return lax.ppermute(value, BLOCK_AXES, moves)


def exchange(pieces, axes):
    return lax.all_to_all(pieces, axes, 0, 0)


def across(value):
    return lax.ppermute(value, "z", [(0, 1), (1, 0)])


def local(queries, keys, values, grads, segment_ids, order):
    z = lax.axis_index("z")
    block = lax.axis_index("b")
    c = lax.axis_index(BLOCK_AXES)
    place = [z, block, 8 * z + 2 * lax.axis_index("y") + block, c]
    info = jnp.concatenate([order, jnp.stack(place).astype(jnp.int32)])
    part = (4, CHUNK // 4, KV_WIDTH)
    whole = (CHUNK, KV_WIDTH)
    own = paired(values, keys)

    here = exchange(own.reshape(8, *part[1:]), SPREAD_AXES).reshape(2, *part)[1]
    there = across(here)
    near_in = move(own, [(0, 1), (1, 2), (2, 3)])
    far_in = move(own, [(0, 2), (1, 3)])
    there, near_in, far_in = lax.optimization_barrier((there, near_in, far_in))
    (pieces,) = route(route_forward_kernel, info, (here, there), (16,))
    arrived = exchange(pieces, PLANE_AXES).reshape(2, 4, 2, *part[1:])
    cross = (arrived[:, :, 0] + arrived[:, :, 1]).reshape(2, *whole)
    pairs = (cross, move(cross, [(1, 0)]), far_in, near_in, own)

    weights, dscores, far_grad, near_grad = scores_and_halo(
        info, segment_ids.reshape(-1, CHUNK), queries, grads, pairs
    )

    before = move(near_grad, [(0, 1)])
    pieces = joined(far_grad, before)
    pieces, weights = lax.optimization_barrier((pieces, weights))
    held = exchange(pieces, PLANE_AXES)
    attended, own_values = output_and_own(0, info, grads, pairs, weights)
    held, own_values = lax.optimization_barrier((held, own_values))
    here, there = route(route_back_kernel, info, (held,), (4, 4))
    there, dscores = lax.optimization_barrier((there, dscores))
    there = across(there)
    grad_query, own_keys = output_and_own(1, info, queries, pairs, dscores)
    near_back = move(near_grad, [(1, 0), (2, 1), (3, 2)])
    far_back = move(far_grad, [(2, 0), (3, 1)])
    pieces = jnp.broadcast_to(here + there, (2, *part)).reshape(8, *part[1:])
    late = exchange(pieces, SPREAD_AXES).reshape(2, *whole)
    late = jnp.where(c >= 2, late, 0)

    early = near_back.astype(jnp.float32) + far_back.astype(jnp.float32)
    value_gradient = own_values + early[0] + late[0].astype(jnp.float32)
    key_gradient = own_keys + early[1] + late[1].astype(jnp.float32)
    return (
        attended,
        grad_query,
        key_gradient.astype(jnp.bfloat16),
        value_gradient.astype(jnp.bfloat16),
    )


def solution(mesh):
    names = ("dp", "z", "y", "b", "x", "core")
    fine = jax.sharding.Mesh(mesh.devices.reshape(-1, 2, 4, 2, 2, 2), names)
    rows = P(names, None)
    return jax.shard_map(
        local,
        mesh=fine,
        in_specs=(rows, rows, rows, rows, P("dp"), P("dp")),
        out_specs=(rows, rows, rows, rows),
        check_vma=False,
    )
```

```python
import functools
import math

import jax
import jax.numpy as jnp
from jax import lax
from jax.experimental import pallas as pl
from jax.experimental.pallas import tpu as pltpu
from jax.sharding import PartitionSpec as P

HEAD_SIZE = 128
QUERY_HEADS = 32
KEY_VALUE_HEADS = 4
GROUP = QUERY_HEADS // KEY_VALUE_HEADS
CHUNK = 128
WINDOW = 3 * CHUNK
KV_WIDTH = KEY_VALUE_HEADS * HEAD_SIZE
BLOCK_AXES = ("x", "core")
SPREAD_AXES = ("x", "y")
PLANE_AXES = ("x", "y", "b")
COUNT = 16


def usable_bias(chunk, segments_ref, bias_ref):
    query_doc = jnp.broadcast_to(segments_ref[pl.ds(chunk, 1), :], (CHUNK, CHUNK))
    for back in (2, 1, 0):
        at = chunk - back
        row = segments_ref[pl.ds(jnp.maximum(at, 0), 1), :]
        row = jnp.where(at >= 0, row, -1)
        usable = jnp.broadcast_to(row, (CHUNK, CHUNK)).T == query_doc
        if back == 0:
            usable &= lax.broadcasted_iota(jnp.int32, (CHUNK, CHUNK), 0) <= (
                lax.broadcasted_iota(jnp.int32, (CHUNK, CHUNK), 1)
            )
        tile = jnp.where(usable, 0.0, -jnp.inf).astype(jnp.float32)
        rows = pl.ds((2 - back) * CHUNK, CHUNK)
        bias_ref[rows, 0:CHUNK] = tile
        bias_ref[rows, CHUNK : 2 * CHUNK] = tile


def stacked(ref, heads):
    return jnp.concatenate(
        [ref[:, a * HEAD_SIZE : (a + 1) * HEAD_SIZE] for a in heads], axis=0
    )


LAST = (((1,), (1,)), ((), ()))
PLAIN = (((1,), (0,)), ((), ()))


def dot(left, right, dims):
    return lax.dot_general(left, right, dims, preferred_element_type=jnp.float32)


def window(info_ref, cross_ref, before_ref, far_ref, near_ref, own_ref):
    chunk = info_ref[COUNT + 3]
    far = jnp.where(chunk < 2, cross_ref[...], far_ref[...])
    near = jnp.where(chunk == 0, before_ref[...], near_ref[...])
    return tuple(jnp.concatenate([far[i], near[i], own_ref[i]], axis=0) for i in range(2))


def score_kernel(
    info_ref,
    segments_ref,
    query_ref,
    grad_ref,
    cross_ref,
    before_ref,
    far_ref,
    near_ref,
    own_ref,
    weight_ref,
    dscore_ref,
    far_grad_ref,
    near_grad_ref,
    bias_ref,
):
    @pl.when(pl.program_id(0) == 0)
    def _():
        usable_bias(info_ref[info_ref[COUNT + 2]] * 4 + info_ref[COUNT + 3], segments_ref, bias_ref)

    scale = 1.0 / math.sqrt(HEAD_SIZE)
    values, keys = window(info_ref, cross_ref, before_ref, far_ref, near_ref, own_ref)
    width = 2 * CHUNK
    pairs = GROUP // 2

    def products(pair):
        heads = (2 * pair, 2 * pair + 1)
        return (
            dot(keys, stacked(query_ref, heads), LAST),
            dot(values, stacked(grad_ref, heads), LAST),
        )

    ahead = products(0)
    for pair in range(pairs):
        scores, dprob = ahead
        if pair + 1 < pairs:
            ahead = products(pair + 1)
        scores = scores + bias_ref[...]
        top = jnp.max(scores, axis=0, keepdims=True)
        raised = jnp.exp2((scores - top) * (scale * math.log2(math.e)))
        share = 1.0 / jnp.sum(raised, axis=0, keepdims=True)
        delta = jnp.sum(raised * dprob, axis=0, keepdims=True) * share
        columns = pl.ds(pair * width, width)
        weight_ref[:, columns] = (raised * share).astype(jnp.bfloat16)
        dscore_ref[:, columns] = (raised * (share * scale) * (dprob - delta)).astype(jnp.bfloat16)
    every = range(GROUP)
    halo = pl.ds(0, 2 * CHUNK)
    grad_keys = dot(dscore_ref[halo, :], stacked(query_ref, every), PLAIN).astype(jnp.bfloat16)
    grad_values = dot(weight_ref[halo, :], stacked(grad_ref, every), PLAIN).astype(jnp.bfloat16)
    for i, total in enumerate((grad_values, grad_keys)):
        far_grad_ref[i] = total[:CHUNK]
        near_grad_ref[i] = total[CHUNK:]


def output_kernel(
    info_ref,
    query_ref,
    grad_ref,
    cross_ref,
    before_ref,
    far_ref,
    near_ref,
    own_ref,
    weight_ref,
    dscore_ref,
    out_ref,
    grad_query_ref,
    own_grad_ref,
):
    values, keys = window(info_ref, cross_ref, before_ref, far_ref, near_ref, own_ref)
    values_t, keys_t = values.T, keys.T
    width = 2 * CHUNK
    for pair in range(GROUP // 2):
        columns = pl.ds(pair * width, width)
        output_t = dot(values_t, weight_ref[:, columns], PLAIN).astype(jnp.bfloat16)
        grad_query_t = dot(keys_t, dscore_ref[:, columns], PLAIN).astype(jnp.bfloat16)
        for i in range(2):
            columns = pl.ds(pair * width + i * CHUNK, CHUNK)
            part = slice(i * CHUNK, (i + 1) * CHUNK)
            out_ref[:, columns] = output_t[:, part].T
            grad_query_ref[:, columns] = grad_query_t[:, part].T
    every = range(GROUP)
    own = pl.ds(2 * CHUNK, CHUNK)
    own_grad_ref[0] = dot(weight_ref[own, :], stacked(grad_ref, every), PLAIN)
    own_grad_ref[1] = dot(dscore_ref[own, :], stacked(query_ref, every), PLAIN)


def attention_specs(rows):
    wide = pl.BlockSpec((rows, GROUP * HEAD_SIZE), lambda g, *_: (0, g))
    pair = pl.BlockSpec((2, rows, HEAD_SIZE), lambda g, *_: (0, 0, g))
    tall = pl.BlockSpec((WINDOW, GROUP * HEAD_SIZE), lambda g, *_: (0, g))
    return wide, pair, tall


def scores_and_halo(info, segments, queries, grads, pairs):
    rows = queries.shape[0]
    wide, pair, tall = attention_specs(rows)
    held = jax.ShapeDtypeStruct((WINDOW, queries.shape[1]), jnp.bfloat16)
    half = jax.ShapeDtypeStruct((2, rows, KV_WIDTH), jnp.bfloat16)
    return pl.pallas_call(
        score_kernel,
        grid_spec=pltpu.PrefetchScalarGridSpec(
            num_scalar_prefetch=1,
            grid=(KEY_VALUE_HEADS,),
            in_specs=[pl.BlockSpec(segments.shape, lambda g, *_: (0, 0)), wide, wide] + [pair] * 5,
            out_specs=[tall, tall, pair, pair],
            scratch_shapes=[pltpu.VMEM((WINDOW, 2 * CHUNK), jnp.float32)],
        ),
        out_shape=[held, held, half, half],
        compiler_params=pltpu.CompilerParams(vmem_limit_bytes=58 * 1024 * 1024),
        cost_estimate=pl.CostEstimate(
            flops=7 * rows * QUERY_HEADS * WINDOW * HEAD_SIZE,
            bytes_accessed=16 * rows * QUERY_HEADS * HEAD_SIZE,
            transcendentals=rows * QUERY_HEADS * WINDOW,
        ),
    )(info, segments, queries, grads, *pairs)


def outputs_and_own(info, queries, grads, pairs, weights, dscores):
    rows = queries.shape[0]
    wide, pair, tall = attention_specs(rows)
    like = jax.ShapeDtypeStruct(queries.shape, jnp.bfloat16)
    return pl.pallas_call(
        output_kernel,
        grid_spec=pltpu.PrefetchScalarGridSpec(
            num_scalar_prefetch=1,
            grid=(KEY_VALUE_HEADS,),
            in_specs=[wide, wide] + [pair] * 5 + [tall, tall],
            out_specs=[wide, wide, pair],
        ),
        out_shape=[like, like, jax.ShapeDtypeStruct((2, rows, KV_WIDTH), jnp.float32)],
        compiler_params=pltpu.CompilerParams(vmem_limit_bytes=58 * 1024 * 1024),
        cost_estimate=pl.CostEstimate(
            flops=5 * rows * QUERY_HEADS * WINDOW * HEAD_SIZE,
            bytes_accessed=20 * rows * QUERY_HEADS * HEAD_SIZE,
            transcendentals=0,
        ),
    )(info, queries, grads, *pairs, weights, dscores)


def slots_in_order(info_ref, slot_ref):
    for j in range(COUNT):
        slot_ref[info_ref[j]] = j


def route_forward_kernel(info_ref, here_ref, there_ref, out_ref, slot_ref):
    slots_in_order(info_ref, slot_ref)
    z, block = info_ref[COUNT], info_ref[COUNT + 1]
    empty = jnp.zeros(out_ref.shape[1:], out_ref.dtype)
    for i in range(8):
        source = slot_ref[lax.rem(info_ref[8 * z + i] + COUNT - 1, COUNT)]
        mine = lax.rem(source, 2) == block
        near = lax.div(source, 8) == z
        y = lax.rem(lax.div(source, 2), 4)
        out_ref[8 + i] = empty

        @pl.when(jnp.logical_and(mine, near))
        def _(i=i, y=y):
            out_ref[i] = here_ref[y]

        @pl.when(jnp.logical_and(mine, jnp.logical_not(near)))
        def _(i=i, y=y):
            out_ref[i] = there_ref[y]

        @pl.when(jnp.logical_not(mine))
        def _(i=i):
            out_ref[i] = empty


def route_back_kernel(info_ref, held_ref, here_ref, there_ref, slot_ref):
    slots_in_order(info_ref, slot_ref)
    z, block = info_ref[COUNT], info_ref[COUNT + 1]
    empty = jnp.zeros(here_ref.shape[1:], here_ref.dtype)
    for half, out_ref in ((z, here_ref), (1 - z, there_ref)):
        for y in range(4):
            after = slot_ref[lax.rem(info_ref[8 * half + 2 * y + block] + 1, COUNT)]
            mine = lax.div(after, 8) == z

            @pl.when(mine)
            def _(out_ref=out_ref, y=y, after=after):
                out_ref[y] = held_ref[lax.rem(after, 8)]

            @pl.when(jnp.logical_not(mine))
            def _(out_ref=out_ref, y=y):
                out_ref[y] = empty


def route(kernel, info, operands, counts):
    shape = operands[0].shape[1:]
    in_vmem = pl.BlockSpec(memory_space=pltpu.VMEM)
    return pl.pallas_call(
        kernel,
        in_specs=[pl.BlockSpec(memory_space=pltpu.SMEM)] + [in_vmem] * len(operands),
        out_specs=[in_vmem] * len(counts),
        out_shape=[jax.ShapeDtypeStruct((n, *shape), jnp.bfloat16) for n in counts],
        scratch_shapes=[pltpu.SMEM((COUNT,), jnp.int32)],
        compiler_params=pltpu.CompilerParams(vmem_limit_bytes=4 * 1024 * 1024),
        cost_estimate=pl.CostEstimate(flops=0, bytes_accessed=1 << 20, transcendentals=0),
    )(info, *operands)


def move(value, moves):
    return lax.ppermute(value, BLOCK_AXES, moves)


def exchange(pieces, axes):
    return lax.all_to_all(pieces, axes, 0, 0)


def across(value):
    return lax.ppermute(value, "z", [(0, 1), (1, 0)])


def local(queries, keys, values, grads, segment_ids, order):
    z = lax.axis_index("z")
    block = lax.axis_index("b")
    c = lax.axis_index(BLOCK_AXES)
    place = [z, block, 8 * z + 2 * lax.axis_index("y") + block, c]
    info = jnp.concatenate([order, jnp.stack(place).astype(jnp.int32)])
    part = (4, CHUNK // 4, KV_WIDTH)
    whole = (CHUNK, KV_WIDTH)
    own = jnp.stack([values, keys], axis=0)

    here = exchange(own.reshape(8, *part[1:]), SPREAD_AXES).reshape(2, *part)[1]
    there = across(here)
    near_in = move(own, [(0, 1), (1, 2), (2, 3)])
    far_in = move(own, [(0, 2), (1, 3)])
    there, near_in, far_in = lax.optimization_barrier((there, near_in, far_in))
    (pieces,) = route(route_forward_kernel, info, (here, there), (16,))
    arrived = exchange(pieces, PLANE_AXES).reshape(2, 4, 2, *part[1:])
    cross = (arrived[:, :, 0] + arrived[:, :, 1]).reshape(2, *whole)
    pairs = (cross, move(cross, [(1, 0)]), far_in, near_in, own)

    weights, dscores, far_grad, near_grad = scores_and_halo(
        info, segment_ids.reshape(-1, CHUNK), queries, grads, pairs
    )

    before = move(near_grad, [(0, 1)])
    twice = lambda t: jnp.broadcast_to(t.reshape(2, 4, 1, *part[1:]), (2, 4, 2, *part[1:]))
    pieces = twice(far_grad).astype(jnp.float32) + twice(before).astype(jnp.float32)
    pieces = pieces.astype(jnp.bfloat16)
    pieces, weights, dscores = lax.optimization_barrier((pieces, weights, dscores))
    held = exchange(pieces.reshape(16, *part[1:]), PLANE_AXES)
    attended, grad_query, own_grad = outputs_and_own(info, queries, grads, pairs, weights, dscores)
    held, own_grad = lax.optimization_barrier((held, own_grad))
    here, there = route(route_back_kernel, info, (held,), (4, 4))
    there, near_grad, far_grad = lax.optimization_barrier((there, near_grad, far_grad))
    there = across(there)
    near_back = move(near_grad, [(1, 0), (2, 1), (3, 2)])
    far_back = move(far_grad, [(2, 0), (3, 1)])
    pieces = jnp.broadcast_to(here + there, (2, *part)).reshape(8, *part[1:])
    late = exchange(pieces, SPREAD_AXES).reshape(2, *whole)
    late = jnp.where(c >= 2, late, 0)

    total = own_grad + near_back.astype(jnp.float32) + far_back.astype(jnp.float32)
    value_gradient = total[0] + late[0].astype(jnp.float32)
    key_gradient = total[1] + late[1].astype(jnp.float32)
    return (
        attended,
        grad_query,
        key_gradient.astype(jnp.bfloat16),
        value_gradient.astype(jnp.bfloat16),
    )


def solution(mesh):
    names = ("dp", "z", "y", "b", "x", "core")
    fine = jax.sharding.Mesh(mesh.devices.reshape(-1, 2, 4, 2, 2, 2), names)
    rows = P(names, None)
    return jax.shard_map(
        local,
        mesh=fine,
        in_specs=(rows, rows, rows, rows, P("dp"), P("dp")),
        out_specs=(rows, rows, rows, rows),
        check_vma=False,
    )
```

```python
import functools
import math

import jax
import jax.numpy as jnp
from jax import lax
from jax.experimental import pallas as pl
from jax.experimental.pallas import tpu as pltpu
from jax.sharding import PartitionSpec as P

HEAD_SIZE = 128
QUERY_HEADS = 32
KEY_VALUE_HEADS = 4
GROUP = QUERY_HEADS // KEY_VALUE_HEADS
CHUNK = 128
WINDOW = 3 * CHUNK
KV_WIDTH = KEY_VALUE_HEADS * HEAD_SIZE
BLOCK_AXES = ("x", "core")
SPREAD_AXES = ("x", "y")
PLANE_AXES = ("x", "y", "b")
COUNT = 16


def usable_bias(chunk, segments_ref, bias_ref):
    query_doc = jnp.broadcast_to(segments_ref[pl.ds(chunk, 1), :], (CHUNK, CHUNK))
    for back in (2, 1, 0):
        at = chunk - back
        row = segments_ref[pl.ds(jnp.maximum(at, 0), 1), :]
        row = jnp.where(at >= 0, row, -1)
        usable = jnp.broadcast_to(row, (CHUNK, CHUNK)).T == query_doc
        if back == 0:
            usable &= lax.broadcasted_iota(jnp.int32, (CHUNK, CHUNK), 0) <= (
                lax.broadcasted_iota(jnp.int32, (CHUNK, CHUNK), 1)
            )
        tile = jnp.where(usable, 0.0, -jnp.inf).astype(jnp.float32)
        rows = pl.ds((2 - back) * CHUNK, CHUNK)
        bias_ref[rows, 0:CHUNK] = tile
        bias_ref[rows, CHUNK : 2 * CHUNK] = tile


def stacked(ref, heads):
    return jnp.concatenate(
        [ref[:, a * HEAD_SIZE : (a + 1) * HEAD_SIZE] for a in heads], axis=0
    )


LAST = (((1,), (1,)), ((), ()))
PLAIN = (((1,), (0,)), ((), ()))


def dot(left, right, dims):
    return lax.dot_general(left, right, dims, preferred_element_type=jnp.float32)


def window(info_ref, cross_ref, before_ref, far_ref, near_ref, own_ref):
    chunk = info_ref[COUNT + 3]
    far = jnp.where(chunk < 2, cross_ref[...], far_ref[...])
    near = jnp.where(chunk == 0, before_ref[...], near_ref[...])
    return tuple(jnp.concatenate([far[i], near[i], own_ref[i]], axis=0) for i in range(2))


def score_kernel(
    info_ref,
    segments_ref,
    query_ref,
    grad_ref,
    cross_ref,
    before_ref,
    far_ref,
    near_ref,
    own_ref,
    weight_ref,
    dscore_ref,
    far_grad_ref,
    near_grad_ref,
    bias_ref,
):
    @pl.when(pl.program_id(0) == 0)
    def _():
        usable_bias(info_ref[info_ref[COUNT + 2]] * 4 + info_ref[COUNT + 3], segments_ref, bias_ref)

    scale = 1.0 / math.sqrt(HEAD_SIZE)
    values, keys = window(info_ref, cross_ref, before_ref, far_ref, near_ref, own_ref)
    width = 2 * CHUNK
    pairs = GROUP // 2

    def products(pair):
        heads = (2 * pair, 2 * pair + 1)
        return (
            dot(keys, stacked(query_ref, heads), LAST),
            dot(values, stacked(grad_ref, heads), LAST),
        )

    ahead = products(0)
    for pair in range(pairs):
        scores, dprob = ahead
        if pair + 1 < pairs:
            ahead = products(pair + 1)
        scores = scores + bias_ref[...]
        top = jnp.max(scores, axis=0, keepdims=True)
        raised = jnp.exp2((scores - top) * (scale * math.log2(math.e)))
        share = 1.0 / jnp.sum(raised, axis=0, keepdims=True)
        delta = jnp.sum(raised * dprob, axis=0, keepdims=True) * share
        columns = pl.ds(pair * width, width)
        weight_ref[:, columns] = (raised * share).astype(jnp.bfloat16)
        dscore_ref[:, columns] = (raised * (share * scale) * (dprob - delta)).astype(jnp.bfloat16)
    every = range(GROUP)
    halo = pl.ds(0, 2 * CHUNK)
    grad_keys = dot(dscore_ref[halo, :], stacked(query_ref, every), PLAIN).astype(jnp.bfloat16)
    grad_values = dot(weight_ref[halo, :], stacked(grad_ref, every), PLAIN).astype(jnp.bfloat16)
    for i, total in enumerate((grad_values, grad_keys)):
        far_grad_ref[i] = total[:CHUNK]
        near_grad_ref[i] = total[CHUNK:]


def output_kernel(
    info_ref,
    query_ref,
    grad_ref,
    cross_ref,
    before_ref,
    far_ref,
    near_ref,
    own_ref,
    weight_ref,
    dscore_ref,
    out_ref,
    grad_query_ref,
    own_grad_ref,
):
    values, keys = window(info_ref, cross_ref, before_ref, far_ref, near_ref, own_ref)
    values_t, keys_t = values.T, keys.T
    width = 2 * CHUNK
    for pair in range(GROUP // 2):
        columns = pl.ds(pair * width, width)
        output_t = dot(values_t, weight_ref[:, columns], PLAIN).astype(jnp.bfloat16)
        grad_query_t = dot(keys_t, dscore_ref[:, columns], PLAIN).astype(jnp.bfloat16)
        for i in range(2):
            columns = pl.ds(pair * width + i * CHUNK, CHUNK)
            part = slice(i * CHUNK, (i + 1) * CHUNK)
            out_ref[:, columns] = output_t[:, part].T
            grad_query_ref[:, columns] = grad_query_t[:, part].T
    every = range(GROUP)
    own = pl.ds(2 * CHUNK, CHUNK)
    own_grad_ref[0] = dot(weight_ref[own, :], stacked(grad_ref, every), PLAIN)
    own_grad_ref[1] = dot(dscore_ref[own, :], stacked(query_ref, every), PLAIN)


def attention_specs(rows):
    wide = pl.BlockSpec((rows, GROUP * HEAD_SIZE), lambda g, *_: (0, g))
    pair = pl.BlockSpec((2, rows, HEAD_SIZE), lambda g, *_: (0, 0, g))
    tall = pl.BlockSpec((WINDOW, GROUP * HEAD_SIZE), lambda g, *_: (0, g))
    return wide, pair, tall


def scores_and_halo(info, segments, queries, grads, pairs):
    rows = queries.shape[0]
    wide, pair, tall = attention_specs(rows)
    held = jax.ShapeDtypeStruct((WINDOW, queries.shape[1]), jnp.bfloat16)
    half = jax.ShapeDtypeStruct((2, rows, KV_WIDTH), jnp.bfloat16)
    return pl.pallas_call(
        score_kernel,
        grid_spec=pltpu.PrefetchScalarGridSpec(
            num_scalar_prefetch=1,
            grid=(KEY_VALUE_HEADS,),
            in_specs=[pl.BlockSpec(segments.shape, lambda g, *_: (0, 0)), wide, wide] + [pair] * 5,
            out_specs=[tall, tall, pair, pair],
            scratch_shapes=[pltpu.VMEM((WINDOW, 2 * CHUNK), jnp.float32)],
        ),
        out_shape=[held, held, half, half],
        compiler_params=pltpu.CompilerParams(vmem_limit_bytes=58 * 1024 * 1024),
        cost_estimate=pl.CostEstimate(
            flops=7 * rows * QUERY_HEADS * WINDOW * HEAD_SIZE,
            bytes_accessed=16 * rows * QUERY_HEADS * HEAD_SIZE,
            transcendentals=rows * QUERY_HEADS * WINDOW,
        ),
    )(info, segments, queries, grads, *pairs)


def outputs_and_own(info, queries, grads, pairs, weights, dscores):
    rows = queries.shape[0]
    wide, pair, tall = attention_specs(rows)
    like = jax.ShapeDtypeStruct(queries.shape, jnp.bfloat16)
    return pl.pallas_call(
        output_kernel,
        grid_spec=pltpu.PrefetchScalarGridSpec(
            num_scalar_prefetch=1,
            grid=(KEY_VALUE_HEADS,),
            in_specs=[wide, wide] + [pair] * 5 + [tall, tall],
            out_specs=[wide, wide, pair],
        ),
        out_shape=[like, like, jax.ShapeDtypeStruct((2, rows, KV_WIDTH), jnp.float32)],
        compiler_params=pltpu.CompilerParams(vmem_limit_bytes=58 * 1024 * 1024),
        cost_estimate=pl.CostEstimate(
            flops=5 * rows * QUERY_HEADS * WINDOW * HEAD_SIZE,
            bytes_accessed=20 * rows * QUERY_HEADS * HEAD_SIZE,
            transcendentals=0,
        ),
    )(info, queries, grads, *pairs, weights, dscores)


def slots_in_order(info_ref, slot_ref):
    for j in range(COUNT):
        slot_ref[info_ref[j]] = j


def route_forward_kernel(info_ref, here_ref, there_ref, out_ref, slot_ref):
    slots_in_order(info_ref, slot_ref)
    z, block = info_ref[COUNT], info_ref[COUNT + 1]
    empty = jnp.zeros(out_ref.shape[1:], out_ref.dtype)
    for i in range(8):
        source = slot_ref[lax.rem(info_ref[8 * z + i] + COUNT - 1, COUNT)]
        mine = lax.rem(source, 2) == block
        near = lax.div(source, 8) == z
        y = lax.rem(lax.div(source, 2), 4)
        out_ref[8 + i] = empty

        @pl.when(jnp.logical_and(mine, near))
        def _(i=i, y=y):
            out_ref[i] = here_ref[y]

        @pl.when(jnp.logical_and(mine, jnp.logical_not(near)))
        def _(i=i, y=y):
            out_ref[i] = there_ref[y]

        @pl.when(jnp.logical_not(mine))
        def _(i=i):
            out_ref[i] = empty


def route_back_kernel(info_ref, held_ref, here_ref, there_ref, slot_ref):
    slots_in_order(info_ref, slot_ref)
    z, block = info_ref[COUNT], info_ref[COUNT + 1]
    empty = jnp.zeros(here_ref.shape[1:], here_ref.dtype)
    for half, out_ref in ((z, here_ref), (1 - z, there_ref)):
        for y in range(4):
            after = slot_ref[lax.rem(info_ref[8 * half + 2 * y + block] + 1, COUNT)]
            mine = lax.div(after, 8) == z

            @pl.when(mine)
            def _(out_ref=out_ref, y=y, after=after):
                out_ref[y] = held_ref[lax.rem(after, 8)]

            @pl.when(jnp.logical_not(mine))
            def _(out_ref=out_ref, y=y):
                out_ref[y] = empty


def route(kernel, info, operands, counts):
    shape = operands[0].shape[1:]
    in_vmem = pl.BlockSpec(memory_space=pltpu.VMEM)
    return pl.pallas_call(
        kernel,
        in_specs=[pl.BlockSpec(memory_space=pltpu.SMEM)] + [in_vmem] * len(operands),
        out_specs=[in_vmem] * len(counts),
        out_shape=[jax.ShapeDtypeStruct((n, *shape), jnp.bfloat16) for n in counts],
        scratch_shapes=[pltpu.SMEM((COUNT,), jnp.int32)],
        compiler_params=pltpu.CompilerParams(vmem_limit_bytes=4 * 1024 * 1024),
        cost_estimate=pl.CostEstimate(flops=0, bytes_accessed=1 << 20, transcendentals=0),
    )(info, *operands)


def move(value, moves):
    return lax.ppermute(value, BLOCK_AXES, moves)


def exchange(pieces, axes):
    return lax.all_to_all(pieces, axes, 0, 0)


def across(value):
    return lax.ppermute(value, "z", [(0, 1), (1, 0)])


def local(queries, keys, values, grads, segment_ids, order):
    z = lax.axis_index("z")
    block = lax.axis_index("b")
    c = lax.axis_index(BLOCK_AXES)
    place = [z, block, 8 * z + 2 * lax.axis_index("y") + block, c]
    info = jnp.concatenate([order, jnp.stack(place).astype(jnp.int32)])
    part = (4, CHUNK // 4, KV_WIDTH)
    whole = (CHUNK, KV_WIDTH)
    own = jnp.stack([values, keys], axis=0)

    here = exchange(own.reshape(8, *part[1:]), SPREAD_AXES).reshape(2, *part)[1]
    there = across(here)
    near_in = move(own, [(0, 1), (1, 2), (2, 3)])
    far_in = move(own, [(0, 2), (1, 3)])
    there, near_in, far_in = lax.optimization_barrier((there, near_in, far_in))
    (pieces,) = route(route_forward_kernel, info, (here, there), (16,))
    arrived = exchange(pieces, PLANE_AXES).reshape(2, 4, 2, *part[1:])
    cross = (arrived[:, :, 0] + arrived[:, :, 1]).reshape(2, *whole)
    pairs = (cross, move(cross, [(1, 0)]), far_in, near_in, own)

    weights, dscores, far_grad, near_grad = scores_and_halo(
        info, segment_ids.reshape(-1, CHUNK), queries, grads, pairs
    )

    before = move(near_grad, [(0, 1)])
    halo = (far_grad.astype(jnp.float32) + before.astype(jnp.float32)).astype(jnp.bfloat16)
    pieces = jnp.broadcast_to(halo.reshape(2, 4, 1, *part[1:]), (2, 4, 2, *part[1:]))
    pieces, weights, dscores = lax.optimization_barrier((pieces, weights, dscores))
    held = exchange(pieces.reshape(16, *part[1:]), PLANE_AXES)
    attended, grad_query, own_grad = outputs_and_own(info, queries, grads, pairs, weights, dscores)
    held, own_grad = lax.optimization_barrier((held, own_grad))
    here, there = route(route_back_kernel, info, (held,), (4, 4))
    there = across(there)
    there, near_grad, far_grad = lax.optimization_barrier((there, near_grad, far_grad))
    near_back = move(near_grad, [(1, 0), (2, 1), (3, 2)])
    far_back = move(far_grad, [(2, 0), (3, 1)])
    pieces = jnp.broadcast_to(here + there, (2, *part)).reshape(8, *part[1:])
    late = exchange(pieces, SPREAD_AXES).reshape(2, *whole)
    late = jnp.where(c >= 2, late, 0)

    total = own_grad + near_back.astype(jnp.float32) + far_back.astype(jnp.float32)
    value_gradient = total[0] + late[0].astype(jnp.float32)
    key_gradient = total[1] + late[1].astype(jnp.float32)
    return (
        attended,
        grad_query,
        key_gradient.astype(jnp.bfloat16),
        value_gradient.astype(jnp.bfloat16),
    )


def solution(mesh):
    names = ("dp", "z", "y", "b", "x", "core")
    fine = jax.sharding.Mesh(mesh.devices.reshape(-1, 2, 4, 2, 2, 2), names)
    rows = P(names, None)
    return jax.shard_map(
        local,
        mesh=fine,
        in_specs=(rows, rows, rows, rows, P("dp"), P("dp")),
        out_specs=(rows, rows, rows, rows),
        check_vma=False,
    )
```

```python
import functools
import math

import jax
import jax.numpy as jnp
from jax import lax
from jax.experimental import pallas as pl
from jax.experimental.pallas import tpu as pltpu
from jax.sharding import PartitionSpec as P

HEAD_SIZE = 128
QUERY_HEADS = 32
KEY_VALUE_HEADS = 4
GROUP = QUERY_HEADS // KEY_VALUE_HEADS
CHUNK = 128
WINDOW = 3 * CHUNK
KV_WIDTH = KEY_VALUE_HEADS * HEAD_SIZE
BLOCK_AXES = ("x", "core")
SPREAD_AXES = ("x", "y")
PLANE_AXES = ("x", "y", "b")
COUNT = 16


def usable_bias(chunk, segments_ref, bias_ref):
    query_doc = jnp.broadcast_to(segments_ref[pl.ds(chunk, 1), :], (CHUNK, CHUNK))
    for back in (2, 1, 0):
        at = chunk - back
        row = segments_ref[pl.ds(jnp.maximum(at, 0), 1), :]
        row = jnp.where(at >= 0, row, -1)
        usable = jnp.broadcast_to(row, (CHUNK, CHUNK)).T == query_doc
        if back == 0:
            usable &= lax.broadcasted_iota(jnp.int32, (CHUNK, CHUNK), 0) <= (
                lax.broadcasted_iota(jnp.int32, (CHUNK, CHUNK), 1)
            )
        tile = jnp.where(usable, 0.0, -jnp.inf).astype(jnp.float32)
        rows = pl.ds((2 - back) * CHUNK, CHUNK)
        bias_ref[rows, 0:CHUNK] = tile
        bias_ref[rows, CHUNK : 2 * CHUNK] = tile


def stacked(ref, heads):
    return jnp.concatenate(
        [ref[:, a * HEAD_SIZE : (a + 1) * HEAD_SIZE] for a in heads], axis=0
    )


LAST = (((1,), (1,)), ((), ()))
PLAIN = (((1,), (0,)), ((), ()))


def dot(left, right, dims):
    return lax.dot_general(left, right, dims, preferred_element_type=jnp.float32)


def window(info_ref, cross_ref, before_ref, far_ref, near_ref, own_ref):
    chunk = info_ref[COUNT + 3]
    far = jnp.where(chunk < 2, cross_ref[...], far_ref[...])
    near = jnp.where(chunk == 0, before_ref[...], near_ref[...])
    return tuple(jnp.concatenate([far[i], near[i], own_ref[i]], axis=0) for i in range(2))


def score_kernel(
    info_ref,
    segments_ref,
    query_ref,
    grad_ref,
    cross_ref,
    before_ref,
    far_ref,
    near_ref,
    own_ref,
    weight_ref,
    dscore_ref,
    far_grad_ref,
    near_grad_ref,
    bias_ref,
):
    @pl.when(pl.program_id(0) == 0)
    def _():
        usable_bias(info_ref[info_ref[COUNT + 2]] * 4 + info_ref[COUNT + 3], segments_ref, bias_ref)

    scale = 1.0 / math.sqrt(HEAD_SIZE)
    values, keys = window(info_ref, cross_ref, before_ref, far_ref, near_ref, own_ref)
    width = 2 * CHUNK
    pairs = GROUP // 2

    def products(pair):
        heads = (2 * pair, 2 * pair + 1)
        return (
            dot(keys, stacked(query_ref, heads), LAST),
            dot(values, stacked(grad_ref, heads), LAST),
        )

    ahead = products(0)
    for pair in range(pairs):
        scores, dprob = ahead
        if pair + 1 < pairs:
            ahead = products(pair + 1)
        scores = scores + bias_ref[...]
        top = jnp.max(scores, axis=0, keepdims=True)
        raised = jnp.exp2((scores - top) * (scale * math.log2(math.e)))
        share = 1.0 / jnp.sum(raised, axis=0, keepdims=True)
        delta = jnp.sum(raised * dprob, axis=0, keepdims=True) * share
        columns = pl.ds(pair * width, width)
        weight_ref[:, columns] = (raised * share).astype(jnp.bfloat16)
        dscore_ref[:, columns] = (raised * (share * scale) * (dprob - delta)).astype(jnp.bfloat16)
    every = range(GROUP)
    halo = pl.ds(0, 2 * CHUNK)
    grad_keys = dot(dscore_ref[halo, :], stacked(query_ref, every), PLAIN).astype(jnp.bfloat16)
    grad_values = dot(weight_ref[halo, :], stacked(grad_ref, every), PLAIN).astype(jnp.bfloat16)
    for i, total in enumerate((grad_values, grad_keys)):
        far_grad_ref[i] = total[:CHUNK]
        near_grad_ref[i] = total[CHUNK:]


def output_kernel(
    info_ref,
    query_ref,
    grad_ref,
    cross_ref,
    before_ref,
    far_ref,
    near_ref,
    own_ref,
    weight_ref,
    dscore_ref,
    out_ref,
    grad_query_ref,
    own_grad_ref,
):
    values, keys = window(info_ref, cross_ref, before_ref, far_ref, near_ref, own_ref)
    values_t, keys_t = values.T, keys.T
    width = 2 * CHUNK
    for pair in range(GROUP // 2):
        columns = pl.ds(pair * width, width)
        output_t = dot(values_t, weight_ref[:, columns], PLAIN).astype(jnp.bfloat16)
        grad_query_t = dot(keys_t, dscore_ref[:, columns], PLAIN).astype(jnp.bfloat16)
        for i in range(2):
            columns = pl.ds(pair * width + i * CHUNK, CHUNK)
            part = slice(i * CHUNK, (i + 1) * CHUNK)
            out_ref[:, columns] = output_t[:, part].T
            grad_query_ref[:, columns] = grad_query_t[:, part].T
    every = range(GROUP)
    own = pl.ds(2 * CHUNK, CHUNK)
    own_grad_ref[0] = dot(weight_ref[own, :], stacked(grad_ref, every), PLAIN)
    own_grad_ref[1] = dot(dscore_ref[own, :], stacked(query_ref, every), PLAIN)


def attention_specs(rows):
    wide = pl.BlockSpec((rows, GROUP * HEAD_SIZE), lambda g, *_: (0, g))
    pair = pl.BlockSpec((2, rows, HEAD_SIZE), lambda g, *_: (0, 0, g))
    tall = pl.BlockSpec((WINDOW, GROUP * HEAD_SIZE), lambda g, *_: (0, g))
    return wide, pair, tall


def scores_and_halo(info, segments, queries, grads, pairs):
    rows = queries.shape[0]
    wide, pair, tall = attention_specs(rows)
    held = jax.ShapeDtypeStruct((WINDOW, queries.shape[1]), jnp.bfloat16)
    half = jax.ShapeDtypeStruct((2, rows, KV_WIDTH), jnp.bfloat16)
    return pl.pallas_call(
        score_kernel,
        grid_spec=pltpu.PrefetchScalarGridSpec(
            num_scalar_prefetch=1,
            grid=(KEY_VALUE_HEADS,),
            in_specs=[pl.BlockSpec(segments.shape, lambda g, *_: (0, 0)), wide, wide] + [pair] * 5,
            out_specs=[tall, tall, pair, pair],
            scratch_shapes=[pltpu.VMEM((WINDOW, 2 * CHUNK), jnp.float32)],
        ),
        out_shape=[held, held, half, half],
        compiler_params=pltpu.CompilerParams(vmem_limit_bytes=55 * 1024 * 1024),
        cost_estimate=pl.CostEstimate(
            flops=7 * rows * QUERY_HEADS * WINDOW * HEAD_SIZE,
            bytes_accessed=16 * rows * QUERY_HEADS * HEAD_SIZE,
            transcendentals=rows * QUERY_HEADS * WINDOW,
        ),
    )(info, segments, queries, grads, *pairs)


def outputs_and_own(info, queries, grads, pairs, weights, dscores):
    rows = queries.shape[0]
    wide, pair, tall = attention_specs(rows)
    like = jax.ShapeDtypeStruct(queries.shape, jnp.bfloat16)
    return pl.pallas_call(
        output_kernel,
        grid_spec=pltpu.PrefetchScalarGridSpec(
            num_scalar_prefetch=1,
            grid=(KEY_VALUE_HEADS,),
            in_specs=[wide, wide] + [pair] * 5 + [tall, tall],
            out_specs=[wide, wide, pair],
        ),
        out_shape=[like, like, jax.ShapeDtypeStruct((2, rows, KV_WIDTH), jnp.float32)],
        compiler_params=pltpu.CompilerParams(vmem_limit_bytes=55 * 1024 * 1024),
        cost_estimate=pl.CostEstimate(
            flops=5 * rows * QUERY_HEADS * WINDOW * HEAD_SIZE,
            bytes_accessed=20 * rows * QUERY_HEADS * HEAD_SIZE,
            transcendentals=0,
        ),
    )(info, queries, grads, *pairs, weights, dscores)


def slots_in_order(info_ref, slot_ref):
    for j in range(COUNT):
        slot_ref[info_ref[j]] = j


def route_forward_kernel(info_ref, here_ref, there_ref, out_ref, slot_ref):
    slots_in_order(info_ref, slot_ref)
    z, block = info_ref[COUNT], info_ref[COUNT + 1]
    empty = jnp.zeros(out_ref.shape[1:], out_ref.dtype)
    for i in range(8):
        source = slot_ref[lax.rem(info_ref[8 * z + i] + COUNT - 1, COUNT)]
        mine = lax.rem(source, 2) == block
        near = lax.div(source, 8) == z
        y = lax.rem(lax.div(source, 2), 4)
        out_ref[8 + i] = empty

        @pl.when(jnp.logical_and(mine, near))
        def _(i=i, y=y):
            out_ref[i] = here_ref[y]

        @pl.when(jnp.logical_and(mine, jnp.logical_not(near)))
        def _(i=i, y=y):
            out_ref[i] = there_ref[y]

        @pl.when(jnp.logical_not(mine))
        def _(i=i):
            out_ref[i] = empty


def route_back_kernel(info_ref, held_ref, here_ref, there_ref, slot_ref):
    slots_in_order(info_ref, slot_ref)
    z, block = info_ref[COUNT], info_ref[COUNT + 1]
    empty = jnp.zeros(here_ref.shape[1:], here_ref.dtype)
    for half, out_ref in ((z, here_ref), (1 - z, there_ref)):
        for y in range(4):
            after = slot_ref[lax.rem(info_ref[8 * half + 2 * y + block] + 1, COUNT)]
            mine = lax.div(after, 8) == z

            @pl.when(mine)
            def _(out_ref=out_ref, y=y, after=after):
                out_ref[y] = held_ref[lax.rem(after, 8)]

            @pl.when(jnp.logical_not(mine))
            def _(out_ref=out_ref, y=y):
                out_ref[y] = empty


def route(kernel, info, operands, counts):
    shape = operands[0].shape[1:]
    in_vmem = pl.BlockSpec(memory_space=pltpu.VMEM)
    return pl.pallas_call(
        kernel,
        in_specs=[pl.BlockSpec(memory_space=pltpu.SMEM)] + [in_vmem] * len(operands),
        out_specs=[in_vmem] * len(counts),
        out_shape=[jax.ShapeDtypeStruct((n, *shape), jnp.bfloat16) for n in counts],
        scratch_shapes=[pltpu.SMEM((COUNT,), jnp.int32)],
        compiler_params=pltpu.CompilerParams(vmem_limit_bytes=4 * 1024 * 1024),
        cost_estimate=pl.CostEstimate(flops=0, bytes_accessed=1 << 20, transcendentals=0),
    )(info, *operands)


def move(value, moves):
    return lax.ppermute(value, BLOCK_AXES, moves)


def exchange(pieces, axes):
    return lax.all_to_all(pieces, axes, 0, 0)


def across(value):
    return lax.ppermute(value, "z", [(0, 1), (1, 0)])


def local(queries, keys, values, grads, segment_ids, order):
    z = lax.axis_index("z")
    block = lax.axis_index("b")
    c = lax.axis_index(BLOCK_AXES)
    place = [z, block, 8 * z + 2 * lax.axis_index("y") + block, c]
    info = jnp.concatenate([order, jnp.stack(place).astype(jnp.int32)])
    part = (4, CHUNK // 4, KV_WIDTH)
    whole = (CHUNK, KV_WIDTH)
    own = jnp.stack([values, keys], axis=0)

    here = exchange(own.reshape(8, *part[1:]), SPREAD_AXES).reshape(2, *part)[1]
    there = across(here)
    near_in = move(own, [(0, 1), (1, 2), (2, 3)])
    far_in = move(own, [(0, 2), (1, 3)])
    there, near_in, far_in = lax.optimization_barrier((there, near_in, far_in))
    (pieces,) = route(route_forward_kernel, info, (here, there), (16,))
    arrived = exchange(pieces, PLANE_AXES).reshape(2, 4, 2, *part[1:])
    cross = (arrived[:, :, 0] + arrived[:, :, 1]).reshape(2, *whole)
    pairs = (cross, move(cross, [(1, 0)]), far_in, near_in, own)

    weights, dscores, far_grad, near_grad = scores_and_halo(
        info, segment_ids.reshape(-1, CHUNK), queries, grads, pairs
    )

    before = move(near_grad, [(0, 1)])
    halo = (far_grad.astype(jnp.float32) + before.astype(jnp.float32)).astype(jnp.bfloat16)
    pieces = jnp.broadcast_to(halo.reshape(2, 4, 1, *part[1:]), (2, 4, 2, *part[1:]))
    pieces, weights, dscores = lax.optimization_barrier((pieces, weights, dscores))
    held = exchange(pieces.reshape(16, *part[1:]), PLANE_AXES)
    attended, grad_query, own_grad = outputs_and_own(info, queries, grads, pairs, weights, dscores)
    held, own_grad = lax.optimization_barrier((held, own_grad))
    here, there = route(route_back_kernel, info, (held,), (4, 4))
    there = across(there)
    near_back = move(near_grad, [(1, 0), (2, 1), (3, 2)])
    far_back = move(far_grad, [(2, 0), (3, 1)])
    pieces = jnp.broadcast_to(here + there, (2, *part)).reshape(8, *part[1:])
    late = exchange(pieces, SPREAD_AXES).reshape(2, *whole)
    late = jnp.where(c >= 2, late, 0)

    total = own_grad + near_back.astype(jnp.float32) + far_back.astype(jnp.float32)
    value_gradient = total[0] + late[0].astype(jnp.float32)
    key_gradient = total[1] + late[1].astype(jnp.float32)
    return (
        attended,
        grad_query,
        key_gradient.astype(jnp.bfloat16),
        value_gradient.astype(jnp.bfloat16),
    )


def solution(mesh):
    names = ("dp", "z", "y", "b", "x", "core")
    fine = jax.sharding.Mesh(mesh.devices.reshape(-1, 2, 4, 2, 2, 2), names)
    rows = P(names, None)
    return jax.shard_map(
        local,
        mesh=fine,
        in_specs=(rows, rows, rows, rows, P("dp"), P("dp")),
        out_specs=(rows, rows, rows, rows),
        check_vma=False,
    )
```
